128 devices in a mesh: row: 8 (over y_lo, z), col: 16 (over x, y_hi, core).
Axes of the slice: x: 4, y: 4 (y_hi: 2, y_lo: 2; y = y_hi * 2 + y_lo), z: 4, core: 2. Of those that a mesh axis runs over, the one named last changes fastest.
Arguments:
- tokens: bfloat16 [1024, 12288], P('col', 'row'), may hold values from -6 to 6
- widen_blocks: bfloat16 [8, 576, 128, 128], P('row', 'col'), may hold values from -0.125 to 0.125
- widen_pattern: int32 [8, 576, 2], P('row', 'col'), may hold values from -1 to 11, as said below
- narrow_blocks: bfloat16 [8, 576, 128, 128], P('row', 'col'), may hold values from -0.078125 to 0.078125
- narrow_pattern: int32 [8, 576, 2], P('row', 'col'), may hold values from -1 to 11, as said below
- cotangent: bfloat16 [1024, 12288], P('col', 'row'), may hold values from -6 to 6
Outputs:
- layer_output: bfloat16 [1024, 12288], P('col', 'row')
- token_grad: bfloat16 [1024, 12288], P('col', 'row')
- widen_grad: bfloat16 [8, 576, 128, 128], P('row', 'col')
- narrow_grad: bfloat16 [8, 576, 128, 128], P('row', 'col')
The draws below stay inside these ranges and needn't reach their ends.
Inputs may be any that keep to these rules, and one draw needn't show every extreme that they name: `widen_pattern`: in each tile the live slots come first and name distinct blocks with entries (r, c), r below 12 and c below 12; the other slots hold -1 in both entries; some tile has all 36 slots live. `narrow_pattern`: in each tile the live slots come first and name distinct blocks with entries (r, c), r below 12 and c below 12; the other slots hold -1 in both entries; some tile has all 36 slots live.
All inputs are finite; a program needn't handle non-finite values.
Results may differ from the reference program's by a relative error of at most 0.028.
Values may be sent and summed in bfloat16 or wider, within the bound.
A program may use at most 128 MiB of HBM per device.

```python
import math
import jax
import jax.numpy as jnp
from jax import lax

D = 12288
FF = 24576
BLK = 128
TOKENS = 1024
DBT = 12
FBT = 12
CAP = 36
N_ROW = 8
N_COL = 16


def tile_pattern(key, in_count, out_count):
    tile_total = N_ROW * N_COL
    number = in_count * out_count
    key_scores, key_counts, key_full = jax.random.split(key, 3)
    scores = jax.random.randint(key_scores, (tile_total, number), 0, 1 << 20) * number
    scores = scores + jnp.arange(number, dtype=jnp.int32)[None, :]
    full_tile = jax.random.randint(key_full, (), 0, tile_total)
    tile_ids = jnp.arange(tile_total, dtype=jnp.int32)
    last_block = jnp.arange(number, dtype=jnp.int32) == number - 1
    scores = jnp.where((tile_ids[:, None] == full_tile) & last_block[None, :], -1, scores)
    ranked = jnp.argsort(scores, axis=1)[:, :CAP].astype(jnp.int32)
    lowest = max(1, CAP // 2)
    filled = jax.random.randint(key_counts, (tile_total,), lowest, CAP + 1)
    filled = jnp.where(tile_ids == full_tile, CAP, filled)
    is_live = jnp.arange(CAP, dtype=jnp.int32)[None, :] < filled[:, None]
    inputs = jnp.where(is_live, ranked // out_count, -1)
    outputs = jnp.where(is_live, ranked % out_count, -1)
    stacked = jnp.stack([inputs, outputs], axis=-1)
    return stacked.reshape(N_ROW, N_COL * CAP, 2).astype(jnp.int32)


def draw_widen_pattern(key, part):
    key = jax.random.fold_in(key, 11)
    return tile_pattern(key, DBT, FBT)


def draw_narrow_pattern(key, part):
    key = jax.random.fold_in(key, 23)
    return tile_pattern(key, FBT, DBT)


def block_scale(key, extent, shards, smallest, largest):
    gain, own = 1.0, jax.random.fold_in(key, 6)
    for dim, shards_of in shards:
        draws = jnp.exp(jax.random.uniform(jax.random.fold_in(own, dim), (shards_of,), jnp.float32, smallest / len(shards), largest / len(shards)))
        gain = gain * jnp.repeat(draws, extent[dim] // shards_of).reshape([-1 if axis == dim else 1 for axis in range(len(extent))])
    return gain


def bell_draw(stream_key, shape, scale, limit, cuts=(), held_as=jnp.bfloat16):
    level = block_scale(stream_key, shape, cuts, -0.22, 0.18) if cuts else 1.0
    values = jax.random.normal(stream_key, shape, jnp.float32) * scale * level
    return jnp.minimum(jnp.maximum(values, -limit), limit).astype(held_as)


def setup_inputs(seed: int = 0) -> dict:
    keys = jax.random.split(jax.random.key(seed), 7)
    return {
        "tokens": bell_draw(keys[0], (TOKENS, D), 1.0, 6.0, ((0, 16), (1, 8))),
        "widen_blocks": bell_draw(keys[1], (N_ROW, N_COL * CAP, BLK, BLK), (D // 5) ** -0.5, 0.125, ((0, 8), (1, 16))),
        "widen_pattern": draw_widen_pattern(jax.random.fold_in(keys[6], 71), 0),
        "narrow_blocks": bell_draw(keys[3], (N_ROW, N_COL * CAP, BLK, BLK), (FF // 5) ** -0.5, 0.078125, ((0, 8), (1, 16))),
        "narrow_pattern": draw_narrow_pattern(jax.random.fold_in(keys[6], 71), 0),
        "cotangent": bell_draw(keys[5], (TOKENS, D), 1.0, 6.0, ((0, 16), (1, 8))),
    }


def gelu_back(pre_value, upstream):
    return jax.vjp(jax.nn.gelu, pre_value)[1](upstream)[0]

def settle(matrix):
    return lax.optimization_barrier(matrix.astype(jnp.bfloat16)).astype(jnp.float32)

def assemble(blocks, pattern, in_count, out_count):
    values = blocks.reshape(N_ROW, N_COL, CAP, BLK, BLK)
    coords = pattern.reshape(N_ROW, N_COL, CAP, 2)
    is_live = coords[..., 0] >= 0
    row_index = jnp.maximum(coords[..., 0], 0).astype(jnp.int32)
    col_index = jnp.maximum(coords[..., 1], 0).astype(jnp.int32)
    masked = jnp.where(is_live[..., None, None], values, jnp.zeros((), values.dtype))

    def place(tile_values, tile_rows, tile_cols):
        canvas = jnp.zeros((in_count, out_count, BLK, BLK), tile_values.dtype)
        canvas = canvas.at[tile_rows, tile_cols].add(tile_values)
        return canvas.transpose(0, 2, 1, 3).reshape(in_count * BLK, out_count * BLK)
    return jax.vmap(jax.vmap(place))(masked, row_index, col_index)

def slot_grads(left, right, pattern, left_on_row, left_count, right_count):
    factor = 1.0 / math.sqrt(TOKENS)
    coords = pattern.reshape(N_ROW * N_COL, CAP, 2)
    left_tiles = left.reshape(TOKENS, -1, left_count, BLK)
    right_tiles = right.reshape(TOKENS, -1, right_count, BLK)

    def one_tile(tile_flat):
        tile_row = tile_flat // N_COL
        tile_col = tile_flat % N_COL
        left_pick = tile_row if left_on_row else tile_col
        right_pick = tile_col if left_on_row else tile_row
        left_part = lax.dynamic_index_in_dim(left_tiles, left_pick, 1, keepdims=False)
        right_part = lax.dynamic_index_in_dim(right_tiles, right_pick, 1, keepdims=False)
        slot_coords = lax.dynamic_index_in_dim(coords, tile_flat, 0, keepdims=False)
        is_live = slot_coords[:, 0] >= 0
        left_picked = jnp.take(left_part, jnp.maximum(slot_coords[:, 0], 0).astype(jnp.int32), axis=1).astype(jnp.float32)
        right_picked = jnp.take(right_part, jnp.maximum(slot_coords[:, 1], 0).astype(jnp.int32), axis=1).astype(jnp.float32)
        summed = jnp.einsum('tcr,tck->crk', left_picked, right_picked)
        return jnp.where(is_live[:, None, None], summed * factor, 0.0).astype(jnp.bfloat16)
    result = lax.map(one_tile, jnp.arange(N_ROW * N_COL, dtype=jnp.int32))
    return result.reshape(N_ROW, N_COL * CAP, BLK, BLK)

def reference(tokens, widen_blocks, widen_pattern, narrow_blocks, narrow_pattern, cotangent):
    model_tile = D // N_ROW
    hidden_tile = FF // N_COL
    widen_tiles = assemble(widen_blocks, widen_pattern, DBT, FBT)
    widen = widen_tiles.transpose(0, 2, 1, 3).reshape(D, FF)
    narrow_tiles = assemble(narrow_blocks, narrow_pattern, FBT, DBT)
    narrow = narrow_tiles.transpose(1, 2, 0, 3).reshape(FF, D)
    hidden = jnp.zeros((TOKENS, FF), jnp.float32)
    hidden_grad = jnp.zeros((TOKENS, FF), jnp.float32)
    for tile_row in range(N_ROW):
        begin_at = tile_row * model_tile
        end_at = begin_at + model_tile
        hidden = hidden + settle(jnp.dot(tokens[:, begin_at:end_at], widen[begin_at:end_at], preferred_element_type=jnp.float32))
        hidden_grad = hidden_grad + settle(jnp.dot(cotangent[:, begin_at:end_at], narrow[:, begin_at:end_at].T, preferred_element_type=jnp.float32))
    activation = jax.nn.gelu(hidden).astype(jnp.bfloat16)
    pre_grad = gelu_back(hidden, hidden_grad).astype(jnp.bfloat16)
    output_sum = jnp.zeros((TOKENS, D), jnp.float32)
    token_sum = jnp.zeros((TOKENS, D), jnp.float32)
    for tile_col in range(N_COL):
        begin_at = tile_col * hidden_tile
        end_at = begin_at + hidden_tile
        output_sum = output_sum + settle(jnp.dot(activation[:, begin_at:end_at], narrow[begin_at:end_at], preferred_element_type=jnp.float32))
        token_sum = token_sum + settle(jnp.dot(pre_grad[:, begin_at:end_at], widen[:, begin_at:end_at].T, preferred_element_type=jnp.float32))
    layer_output = output_sum.astype(jnp.bfloat16)
    token_grad = token_sum.astype(jnp.bfloat16)
    widen_grad = slot_grads(tokens, pre_grad, widen_pattern, True, DBT, FBT)
    narrow_grad = slot_grads(activation, cotangent, narrow_pattern, False, FBT, DBT)
    return (layer_output, token_grad, widen_grad, narrow_grad)
```

```python
import functools

import jax
import jax.numpy as jnp
from jax import lax
from jax.experimental import pallas as pl
from jax.experimental.pallas import tpu as pltpu
from jax.sharding import PartitionSpec as P

MESH = pl.DeviceIdType.MESH
BLK = 128
TILE = 12
SIDE = BLK * TILE
CAP = 36
TOKENS = 1024
STAGES = 4
ROWS = TOKENS // STAGES
ROW_SHARE = ROWS // 8
COL_SHARE = ROWS // 16
WIDE = 512
CURVE = 0.7978845608028654
CUBIC = 0.044715
PLAIN = (((1,), (0,)), ((), ()))
FLIPPED = (((1,), (1,)), ((), ()))
TALL = (((0,), (0,)), ((), ()))
COL_GATHER, CORE_GATHER, ROW_SUM, ROW_GATHER, CORE_SUM, COL_SUM, COPIES = 0, 7, 8, 15, 22, 23, 30


def plan():
    order = [("assemble", 0, 0)]
    waiting = []
    chain = (
        "gather_mid", "gather_pass", "gather_core", "rise", "sum_mid", "sum_pair", "sum_end",
        "spread_mid", "spread_pass", "spread_end", "fall", "core_end", "out_mid", "out_pair", "out_end",
    )
    for s in range(STAGES):
        for a in range(2):
            waiting.append((s, a))
    begun = {}
    order.append(("gather", 0, 0))
    order.append(("gather", 0, 1))
    order.append(("assemble", 0, 1))
    for index, (s, a) in enumerate(waiting):
        for depth, name in enumerate(chain):
            begun[(index * 4 + depth, index, depth)] = (name, s, a)
    for key in sorted(begun):
        name, s, a = begun[key]
        if name == "gather_mid" and s + 1 < STAGES:
            order.append((name, s, a))
            order.append(("gather", s + 1, a))
        else:
            order.append((name, s, a))
        if name == "rise":
            order.append(("flip", s, a))
        if name == "spread_end" and s == STAGES - 1:
            order.append(("slots", 0, a))
    return order


def body(
    places, widen_at, narrow_at, tokens, cotangent, widen_blocks, narrow_blocks,
    layer_output, token_grad, widen_grad, narrow_grad,
    gathered, terms, fields, tiles, row_one, row_two, row_pair, row_send, core_in,
    col_one, col_two, col_pair, col_send, hidden, spare, flipped, dense, send_sem, recv_sem,
):
    row, col = lax.axis_index("row"), lax.axis_index("col")
    y_lo, z = row // 4, row % 4
    x, y_hi, core = col // 4, (col // 2) % 2, col % 2

    def on_row(pair, ring):
        return (pair * 4 + ring % 4, col)

    def on_col(ring, pair, side):
        return (row, (ring % 4) * 4 + pair * 2 + side)

    z_next, z_back, y_near = on_row(y_lo, z + 1), on_row(y_lo, z + 3), on_row(1 - y_lo, z)
    x_next, x_back = on_col(x + 1, y_hi, core), on_col(x + 3, y_hi, core)
    y_far, other_core = on_col(x, 1 - y_hi, core), on_col(x, y_hi, 1 - core)

    barrier = pltpu.get_barrier_semaphore()
    partners = (z_next, z_back, y_near, x_next, x_back, y_far, other_core)
    for partner in partners:
        pl.semaphore_signal(barrier, inc=1, device_id=partner, device_id_type=MESH)
    pl.semaphore_wait(barrier, len(partners))

    copies = {}

    def send(s, a, k, source, target, device):
        copy = pltpu.make_async_remote_copy(
            src_ref=source, dst_ref=target, send_sem=send_sem.at[a, s, k], recv_sem=recv_sem.at[a, s, k],
            device_id=device, device_id_type=MESH,
        )
        copy.start()
        copies[s, a, k] = copy

    def arrived(s, a, *ks):
        for k in ks:
            copies[s, a, k].wait_recv()

    def span(ref, a, s, start, length):
        return ref.at[a, s, pl.ds(pl.multiple_of(start, length), length)]

    class Ring:
        def __init__(self, place, pair, share, base, ahead, behind, partner):
            self.place, self.pair, self.share, self.base = place, pair, share, base
            self.ahead, self.behind, self.partner = ahead, behind, partner

        def piece(self, ref, a, s, step, pair):
            return span(ref, a, s, self.base + (((self.place + step) % 4) * 2 + pair) * self.share, self.share)

        def spread(self, ref, s, a, k):
            own = self.piece(ref, a, s, 0, self.pair)
            send(s, a, k, own, own, self.partner)
            send(s, a, k + 1, own, own, self.ahead)
            send(s, a, k + 2, own, own, self.behind)

        def spread_mid(self, ref, s, a, k):
            arrived(s, a, k)
            near = self.piece(ref, a, s, 0, 1 - self.pair)
            send(s, a, k + 3, near, near, self.ahead)
            send(s, a, k + 4, near, near, self.behind)

        def spread_pass(self, ref, s, a, k):
            arrived(s, a, k + 1)
            left = self.piece(ref, a, s, 3, self.pair)
            send(s, a, k + 5, left, left, self.ahead)
            arrived(s, a, k + 4)
            right = self.piece(ref, a, s, 1, 1 - self.pair)
            send(s, a, k + 6, right, right, self.behind)

        def spread_end(self, s, a, k):
            arrived(s, a, k + 2, k + 3, k + 5, k + 6)

        def total(self, ref, one, two, s, a, k):
            size = self.share
            send(s, a, k, self.piece(ref, a, s, 2, 0), span(one, a, s, 0, size), self.ahead)
            send(s, a, k + 1, self.piece(ref, a, s, 2, 1), span(one, a, s, size, size), self.behind)
            send(s, a, k + 2, self.piece(ref, a, s, 1, 1), span(two, a, s, size, size), self.ahead)
            send(s, a, k + 3, self.piece(ref, a, s, 3, 0), span(two, a, s, 2 * size, size), self.behind)

        def total_mid(self, ref, one, two, s, a, k):
            size = self.share
            arrived(s, a, k)
            there = self.piece(ref, a, s, 1, 0)
            add_into(there, [there, span(one, a, s, 0, size)], size)
            send(s, a, k + 4, there, span(two, a, s, 0, size), self.ahead)
            arrived(s, a, k + 1)
            there = self.piece(ref, a, s, 3, 1)
            add_into(there, [there, span(one, a, s, size, size)], size)
            send(s, a, k + 5, there, span(two, a, s, 3 * size, size), self.behind)

        def addends(self, ref, two, s, a, pair):
            size = self.share
            return [
                self.piece(ref, a, s, 0, pair), span(two, a, s, pair * size, size),
                span(two, a, s, (2 + pair) * size, size),
            ]

        def total_pair(self, ref, two, outgoing, incoming, s, a, k):
            arrived(s, a, k + 2, k + 3, k + 4, k + 5)
            add_into(outgoing.at[a, s], self.addends(ref, two, s, a, 1 - self.pair), self.share)
            send(s, a, k + 6, outgoing.at[a, s], incoming.at[a, s], self.partner)

        def total_end(self, ref, two, incoming, s, a, k):
            arrived(s, a, k + 6)
            return self.addends(ref, two, s, a, self.pair) + [incoming.at[a, s]]

    def add_into(target, refs, count):
        @pl.loop(0, count // 16)
        def _(i):
            part = pl.ds(pl.multiple_of(i * 16, 16), 16)
            value = refs[0][part].astype(jnp.float32)
            for ref in refs[1:]:
                value = value + ref[part].astype(jnp.float32)
            target[part] = value.astype(target.dtype)

    row_ring = Ring(z, y_lo, ROW_SHARE, 0, z_next, z_back, y_near)
    col_ring = Ring(x, y_hi, COL_SHARE, core * (ROWS // 2), x_next, x_back, y_far)
    inputs, outputs = (tokens, cotangent), (layer_output, token_grad)

    def product(source, tile, dims, target):
        @pl.loop(0, SIDE // WIDE)
        def _(j):
            part = pl.ds(pl.multiple_of(j * WIDE, WIDE), WIDE)
            other = tiles[tile, :, part] if dims is PLAIN else tiles[tile, part, :]
            target[:, part] = lax.dot_general(
                source[...], other, dims, preferred_element_type=jnp.float32
            ).astype(jnp.bfloat16)

    def assemble(s, a):
        blocks = (widen_blocks, narrow_blocks)[a]
        spare[CAP] = jnp.zeros((BLK, BLK), jnp.bfloat16)

        @pl.loop(0, CAP)
        def _(i):
            spare[i] = blocks[0, i]

        @pl.loop(0, TILE)
        def _(i):
            for j in range(TILE):
                tiles[a, pl.ds(pl.multiple_of(i * BLK, BLK), BLK), j * BLK:(j + 1) * BLK] = spare[
                    places[a, i * TILE + j]
                ]

    def gather(s, a):
        own = col_ring.piece(gathered, a, s, 0, y_hi)
        own[...] = inputs[a][s * COL_SHARE:(s + 1) * COL_SHARE]
        col_ring.spread(gathered, s, a, COL_GATHER)

    def gather_mid(s, a):
        col_ring.spread_mid(gathered, s, a, COL_GATHER)

    def gather_pass(s, a):
        col_ring.spread_pass(gathered, s, a, COL_GATHER)

    def gather_core(s, a):
        col_ring.spread_end(s, a, COL_GATHER)
        half = span(gathered, a, s, core * (ROWS // 2), ROWS // 2)
        send(s, a, CORE_GATHER, half, half, other_core)

    def rise(s, a):
        arrived(s, a, CORE_GATHER)
        product(gathered.at[a, s], a, (PLAIN, FLIPPED)[a], terms.at[a, s])
        row_ring.total(terms, row_one, row_two, s, a, ROW_SUM)

    def sum_mid(s, a):
        row_ring.total_mid(terms, row_one, row_two, s, a, ROW_SUM)

    def sum_pair(s, a):
        row_ring.total_pair(terms, row_two, row_send, row_pair, s, a, ROW_SUM)

    def sum_end(s, a):
        refs = row_ring.total_end(terms, row_two, row_pair, s, a, ROW_SUM)
        own = row_ring.piece(fields, a, s, 0, y_lo)

        @pl.loop(0, ROW_SHARE // 16)
        def _(i):
            part = pl.ds(pl.multiple_of(i * 16, 16), 16)
            value = refs[0][part].astype(jnp.float32)
            for ref in refs[1:]:
                value = value + ref[part].astype(jnp.float32)
            if a == 0:
                hidden[s, part] = value
                bend = jnp.tanh(CURVE * (value + CUBIC * (value * value * value)))
                own[part] = (0.5 * value * (1.0 + bend)).astype(jnp.bfloat16)
            else:
                at = hidden[s, part]
                square = at * at
                bend = jnp.tanh(CURVE * (at + CUBIC * (square * at)))
                slope = 0.5 * (1.0 + bend) + 0.5 * at * (1.0 - bend * bend) * CURVE * (1.0 + 3.0 * CUBIC * square)
                own[part] = (slope * value).astype(jnp.bfloat16)

        row_ring.spread(fields, s, a, ROW_GATHER)

    def spread_mid(s, a):
        row_ring.spread_mid(fields, s, a, ROW_GATHER)

    def spread_pass(s, a):
        row_ring.spread_pass(fields, s, a, ROW_GATHER)

    def spread_end(s, a):
        row_ring.spread_end(s, a, ROW_GATHER)

    def fall(s, a):
        for k in range(ROW_SUM, ROW_SUM + 6):
            copies.pop((s, a, k)).wait_send()
        product(fields.at[a, s], 1 - a, (PLAIN, FLIPPED)[a], terms.at[a, s])
        half = span(terms, a, s, (1 - core) * (ROWS // 2), ROWS // 2)
        send(s, a, CORE_SUM, half, core_in.at[a, s], other_core)

    def core_end(s, a):
        arrived(s, a, CORE_SUM)
        half = span(terms, a, s, core * (ROWS // 2), ROWS // 2)
        add_into(half, [half, core_in.at[a, s]], ROWS // 2)
        col_ring.total(terms, col_one, col_two, s, a, COL_SUM)

    def out_mid(s, a):
        col_ring.total_mid(terms, col_one, col_two, s, a, COL_SUM)

    def out_pair(s, a):
        col_ring.total_pair(terms, col_two, col_send, col_pair, s, a, COL_SUM)

    def out_end(s, a):
        refs = col_ring.total_end(terms, col_two, col_pair, s, a, COL_SUM)
        add_into(outputs[a].at[pl.ds(s * COL_SHARE, COL_SHARE)], refs, COL_SHARE)

    def flip(s, a):
        source = gathered.at[a, s]

        @pl.loop(0, TILE)
        def _(i):
            part = pl.ds(pl.multiple_of(i * BLK, BLK), BLK)
            flipped[a, part, s * ROWS:(s + 1) * ROWS] = source[:, part].T

    def slots(s, a):
        at, target = (narrow_at, widen_at)[a], (narrow_grad, widen_grad)[a]
        dense[TILE * TILE] = jnp.zeros((BLK, BLK), jnp.bfloat16)

        @pl.loop(0, SIDE // WIDE)
        def _(j):
            part = pl.ds(pl.multiple_of(j * WIDE, WIDE), WIDE)
            right = fields[a, :, :, part].reshape(TOKENS, WIDE)

            @pl.loop(0, SIDE // WIDE)
            def _(i):
                value = lax.dot_general(
                    flipped[1 - a, pl.ds(pl.multiple_of(i * WIDE, WIDE), WIDE), :], right, PLAIN,
                    preferred_element_type=jnp.float32,
                )
                value = (value * (1.0 / 32.0)).astype(jnp.bfloat16)
                for r in range(WIDE // BLK):
                    for c in range(WIDE // BLK):
                        place = (i * (WIDE // BLK) + r) * TILE + j * (WIDE // BLK) + c
                        dense[place] = value[r * BLK:(r + 1) * BLK, c * BLK:(c + 1) * BLK]

        @pl.loop(0, CAP // 4)
        def _(g):
            for u in range(4):
                block = dense[at[g * 4 + u]]
                target[0, g * 4 + u] = block.T if a == 0 else block

    steps = {
        step.__name__: step
        for step in (
            assemble, gather, gather_mid, gather_pass, gather_core, rise, sum_mid, sum_pair, sum_end, spread_mid,
            spread_pass, spread_end, fall, core_end, out_mid, out_pair, out_end, flip, slots,
        )
    }
    for name, s, a in plan():
        steps[name](s, a)
    for copy in copies.values():
        copy.wait_send()


def local(tokens, widen_blocks, widen_pattern, narrow_blocks, narrow_pattern, cotangent):
    pattern = jnp.stack([widen_pattern[0], narrow_pattern[0]])
    flat = jnp.where(pattern[..., 0] >= 0, pattern[..., 0] * TILE + pattern[..., 1], -1)
    match = flat[:, :, None] == jnp.arange(TILE * TILE, dtype=jnp.int32)
    slot = jnp.arange(CAP, dtype=jnp.int32)[None, :, None]
    places = jnp.min(jnp.where(match, slot, CAP), axis=1)
    blocks = jnp.where(pattern[..., 0] >= 0, jnp.stack([flat[0], pattern[1, :, 1] * TILE + pattern[1, :, 0]]), TILE * TILE)
    vmem, smem = pl.BlockSpec(memory_space=pltpu.VMEM), pl.BlockSpec(memory_space=pltpu.SMEM)

    def room(*shape, dtype=jnp.bfloat16):
        return pltpu.VMEM((*shape, SIDE), dtype)

    outs = pl.pallas_call(
        body,
        out_shape=(
            jax.ShapeDtypeStruct(tokens.shape, jnp.bfloat16),
            jax.ShapeDtypeStruct(tokens.shape, jnp.bfloat16),
            jax.ShapeDtypeStruct(widen_blocks.shape, jnp.bfloat16),
            jax.ShapeDtypeStruct(narrow_blocks.shape, jnp.bfloat16),
        ),
        in_specs=[smem] * 3 + [vmem] * 4,
        out_specs=[vmem] * 4,
        scratch_shapes=[
            room(2, STAGES, ROWS),
            room(2, STAGES, ROWS),
            room(2, STAGES, ROWS),
            room(2, SIDE),
            room(2, STAGES, 2 * ROW_SHARE),
            room(2, STAGES, 4 * ROW_SHARE),
            room(2, STAGES, ROW_SHARE),
            room(2, STAGES, ROW_SHARE),
            room(2, STAGES, ROWS // 2),
            room(2, STAGES, 2 * COL_SHARE),
            room(2, STAGES, 4 * COL_SHARE),
            room(2, STAGES, COL_SHARE),
            room(2, STAGES, COL_SHARE),
            room(STAGES, ROW_SHARE, dtype=jnp.float32),
            pltpu.VMEM((CAP + 1, BLK, BLK), jnp.bfloat16),
            pltpu.VMEM((2, SIDE, TOKENS), jnp.bfloat16),
            pltpu.VMEM((TILE * TILE + 1, BLK, BLK), jnp.bfloat16),
            pltpu.SemaphoreType.DMA((2, STAGES, COPIES)),
            pltpu.SemaphoreType.DMA((2, STAGES, COPIES)),
        ],
        compiler_params=pltpu.CompilerParams(
            collective_id=0, has_side_effects=True, vmem_limit_bytes=62 * 2**20
        ),
        name="layer",
    )(
        places, blocks[0], blocks[1], tokens, cotangent, widen_blocks, narrow_blocks,
    )
    return outs


def solution(mesh):
    placed = (
        P("col", "row"),
        P("row", "col", None, None),
        P("row", "col", None),
        P("row", "col", None, None),
        P("row", "col", None),
        P("col", "row"),
    )
    return jax.shard_map(
        local,
        mesh=mesh,
        in_specs=placed,
        out_specs=(
            P("col", "row"),
            P("col", "row"),
            P("row", "col", None, None),
            P("row", "col", None, None),
        ),
        check_vma=False,
    )
```

```python
import functools

import jax
import jax.numpy as jnp
from jax import lax
from jax.experimental import pallas as pl
from jax.experimental.pallas import tpu as pltpu
from jax.sharding import PartitionSpec as P

MESH = pl.DeviceIdType.MESH
BLK = 128
TILE = 12
SIDE = BLK * TILE
CAP = 36
TOKENS = 1024
STAGES = 4
ROWS = TOKENS // STAGES
ROW_SHARE = ROWS // 8
COL_SHARE = ROWS // 16
WIDE = 512
CURVE = 0.7978845608028654
CUBIC = 0.044715
PLAIN = (((1,), (0,)), ((), ()))
FLIPPED = (((1,), (1,)), ((), ()))
TALL = (((0,), (0,)), ((), ()))
COL_GATHER, CORE_GATHER, ROW_SUM, ROW_GATHER, CORE_SUM, COL_SUM, COPIES = 0, 7, 8, 18, 26, 27, 34


NEAR = ((0, 0), (0, 1), (2, 0))
WIDE_FIRST = ((0, 0), (0, 1), (1, 0))
STEPS = (
    "gather", "assemble", "gather_mid", "gather_pass", "gather_core", "rise", "sumb_two", "sum_mid", "sumb_one",
    "sumb_mid", "sum_pair", "sumb_end", "sum_end", "sprb_mid", "flip", "sprb_pass", "spread_mid", "sprb_end", "fall",
    "spread_pass", "core_end", "out_mid", "spread_end", "out_pair", "slot", "out_end", "pick",
)
ORDER = (
    (0, 0, 0), (0, 1, 0), (1, 0, 0), (0, 2, 0), (2, 0, 0), (2, 1, 0), (2, 2, 0), (0, 3, 0), (3, 0, 0), (3, 1, 0),
    (2, 3, 0), (3, 2, 0), (0, 0, 1), (1, 0, 1), (4, 0, 0), (0, 1, 1), (4, 1, 0), (3, 3, 0), (5, 0, 0), (4, 2, 0),
    (5, 1, 0), (4, 3, 0), (0, 2, 1), (0, 3, 1), (5, 2, 0), (6, 0, 0), (2, 1, 1), (7, 1, 0), (2, 0, 1), (5, 3, 0),
    (3, 0, 1), (8, 0, 0), (3, 1, 1), (9, 0, 0), (10, 1, 0), (2, 2, 1), (4, 0, 1), (7, 3, 0), (3, 2, 1), (6, 2, 0),
    (2, 3, 1), (5, 0, 1), (4, 2, 1), (8, 2, 0), (11, 0, 0), (10, 3, 0), (9, 2, 0), (5, 2, 1), (12, 1, 0), (13, 0, 0),
    (3, 3, 1), (11, 2, 0), (14, 0, 1), (6, 0, 1), (4, 3, 1), (7, 2, 1), (4, 1, 1), (14, 3, 0), (8, 0, 1), (5, 3, 1),
    (13, 1, 0), (5, 1, 1), (14, 1, 1), (12, 3, 0), (9, 0, 1), (14, 1, 0), (10, 2, 1), (14, 3, 1), (14, 0, 0),
    (14, 2, 0), (14, 2, 1), (7, 3, 1), (15, 0, 0), (16, 2, 0), (15, 1, 0), (7, 1, 1), (16, 3, 0), (11, 0, 1),
    (12, 2, 1), (10, 3, 1), (17, 0, 0), (18, 0, 0), (19, 2, 0), (17, 1, 0), (18, 1, 0), (10, 1, 1), (20, 0, 0),
    (19, 3, 0), (16, 2, 1), (20, 1, 0), (21, 0, 0), (12, 3, 1), (13, 0, 1), (21, 1, 0), (12, 1, 1), (22, 2, 0),
    (18, 2, 0), (23, 0, 0), (22, 3, 0), (18, 3, 0), (19, 2, 1), (20, 2, 0), (16, 3, 1), (24, 0, 0), (20, 3, 0),
    (15, 0, 1), (21, 2, 0), (16, 1, 1), (25, 0, 0), (23, 1, 0), (24, 1, 0), (22, 2, 1), (18, 2, 1), (23, 2, 0),
    (17, 0, 1), (18, 0, 1), (19, 1, 1), (19, 3, 1), (20, 2, 1), (21, 3, 0), (24, 2, 0), (20, 0, 1), (21, 2, 1),
    (22, 1, 1), (18, 1, 1), (22, 3, 1), (18, 3, 1), (21, 0, 1), (23, 3, 0), (20, 1, 1), (23, 2, 1), (26, 0, 0),
    (20, 3, 1), (24, 0, 1), (25, 3, 0), (21, 1, 1), (21, 3, 1), (25, 1, 0), (23, 0, 1), (24, 1, 1), (23, 1, 1),
    (23, 3, 1), (24, 2, 1), (25, 0, 1), (25, 2, 0), (25, 2, 1), (25, 1, 1), (26, 0, 1), (25, 3, 1),
)


def body(
    places, widen_at, narrow_at, tokens, cotangent, widen_blocks, narrow_blocks,
    layer_output, token_grad, widen_grad, narrow_grad,
    gathered, terms, fields, tiles, row_one, row_two, row_pair, row_send, core_in,
    col_one, col_two, col_pair, col_send, hidden, spare, flipped, dense, send_sem, recv_sem,
):
    row, col = lax.axis_index("row"), lax.axis_index("col")
    y_lo, z = row // 4, row % 4
    x, y_hi, core = col // 4, (col // 2) % 2, col % 2

    def on_row(pair, ring):
        return (pair * 4 + ring % 4, col)

    def on_col(ring, pair, side):
        return (row, (ring % 4) * 4 + pair * 2 + side)

    z_next, z_back, y_near = on_row(y_lo, z + 1), on_row(y_lo, z + 3), on_row(1 - y_lo, z)
    x_next, x_back = on_col(x + 1, y_hi, core), on_col(x + 3, y_hi, core)
    y_far, other_core = on_col(x, 1 - y_hi, core), on_col(x, y_hi, 1 - core)

    barrier = pltpu.get_barrier_semaphore()
    partners = (z_next, z_back, y_near, x_next, x_back, y_far, other_core)
    for partner in partners:
        pl.semaphore_signal(barrier, inc=1, device_id=partner, device_id_type=MESH)
    pl.semaphore_wait(barrier, len(partners))

    copies = {}

    def send(s, a, k, source, target, device):
        copy = pltpu.make_async_remote_copy(
            src_ref=source, dst_ref=target, send_sem=send_sem.at[a, s, k], recv_sem=recv_sem.at[a, s, k],
            device_id=device, device_id_type=MESH,
        )
        copy.start()
        copies[s, a, k] = copy

    def arrived(s, a, *ks):
        for k in ks:
            copies[s, a, k].wait_recv()

    def span(ref, a, s, start, length):
        return ref.at[a, s, pl.ds(pl.multiple_of(start, length), length)]

    class Ring:
        def __init__(self, place, pair, share, base, ahead, behind, partner):
            self.place, self.pair, self.share, self.base = place, pair, share, base
            self.ahead, self.behind, self.partner = ahead, behind, partner

        def piece(self, ref, a, s, step, pair):
            return span(ref, a, s, self.base + (((self.place + step) % 4) * 2 + pair) * self.share, self.share)

        def spread(self, ref, s, a, k):
            own = self.piece(ref, a, s, 0, self.pair)
            send(s, a, k, own, own, self.partner)
            send(s, a, k + 1, own, own, self.ahead)
            send(s, a, k + 2, own, own, self.behind)

        def spread_mid(self, ref, s, a, k):
            arrived(s, a, k)
            near = self.piece(ref, a, s, 0, 1 - self.pair)
            send(s, a, k + 3, near, near, self.ahead)
            send(s, a, k + 4, near, near, self.behind)

        def spread_pass(self, ref, s, a, k):
            arrived(s, a, k + 1)
            left = self.piece(ref, a, s, 3, self.pair)
            send(s, a, k + 5, left, left, self.ahead)
            arrived(s, a, k + 4)
            right = self.piece(ref, a, s, 1, 1 - self.pair)
            send(s, a, k + 6, right, right, self.behind)

        def spread_end(self, s, a, k):
            arrived(s, a, k + 2, k + 3, k + 5, k + 6)

        def half(self, ref, which):
            size = self.share // 2
            return ref.at[pl.ds(which * size, size)]

        def wide(self, ref, s, a, k):
            own = self.piece(ref, a, s, 0, self.pair)
            send(s, a, k, own, own, self.ahead)
            send(s, a, k + 1, own, own, self.behind)
            send(s, a, k + 4, own, own, self.partner)

        def wide_mid(self, ref, s, a, k):
            left, right = self.piece(ref, a, s, 3, self.pair), self.piece(ref, a, s, 1, self.pair)
            arrived(s, a, k)
            send(s, a, k + 2, self.half(left, 0), self.half(left, 0), self.ahead)
            arrived(s, a, k + 1)
            send(s, a, k + 3, self.half(right, 1), self.half(right, 1), self.behind)
            send(s, a, k + 5, left, left, self.partner)
            send(s, a, k + 6, right, right, self.partner)

        def wide_pass(self, ref, s, a, k):
            arrived(s, a, k + 2, k + 3)
            far = self.piece(ref, a, s, 2, self.pair)
            send(s, a, k + 7, far, far, self.partner)

        def wide_end(self, s, a, k):
            arrived(s, a, k + 4, k + 5, k + 6, k + 7)

        def near(self, ref, near, s, a, k):
            for i, step in enumerate((2, 1, 3, 0)):
                source = self.piece(ref, a, s, step, 1 - self.pair)
                send(s, a, k + i, source, span(near, a, s, step * self.share, self.share), self.partner)

        def join(self, ref, near, s, a, step):
            there = self.piece(ref, a, s, step, self.pair)
            add_into(there, [there, span(near, a, s, step * self.share, self.share)], self.share)
            return there

        def near_two(self, ref, near, one, s, a, k):
            arrived(s, a, k)
            there = self.join(ref, near, s, a, 2)
            send(s, a, k + 4, self.half(there, 0), self.half(one.at[a, s], 0), self.ahead)
            send(s, a, k + 5, self.half(there, 1), self.half(one.at[a, s], 1), self.behind)

        def near_one(self, ref, near, two, s, a, k):
            size = self.share
            arrived(s, a, k + 1)
            there = self.join(ref, near, s, a, 1)
            send(s, a, k + 6, self.half(there, 1), self.half(span(two, a, s, 0, size), 1), self.ahead)
            arrived(s, a, k + 2)
            there = self.join(ref, near, s, a, 3)
            send(s, a, k + 7, self.half(there, 0), self.half(span(two, a, s, size, size), 0), self.behind)

        def near_mid(self, ref, one, two, s, a, k):
            size = self.share
            arrived(s, a, k + 4)
            there = self.half(self.piece(ref, a, s, 1, self.pair), 0)
            add_into(there, [there, self.half(one.at[a, s], 0)], size // 2)
            send(s, a, k + 8, there, self.half(span(two, a, s, 0, size), 0), self.ahead)
            arrived(s, a, k + 5)
            there = self.half(self.piece(ref, a, s, 3, self.pair), 1)
            add_into(there, [there, self.half(one.at[a, s], 1)], size // 2)
            send(s, a, k + 9, there, self.half(span(two, a, s, size, size), 1), self.behind)

        def near_end(self, ref, near, two, s, a, k):
            size = self.share
            arrived(s, a, k + 3, k + 6, k + 7, k + 8, k + 9)
            return [
                self.piece(ref, a, s, 0, self.pair), span(near, a, s, 0, size),
                span(two, a, s, 0, size), span(two, a, s, size, size),
            ]

        def total(self, ref, one, two, s, a, k):
            size = self.share
            send(s, a, k, self.piece(ref, a, s, 2, 0), span(one, a, s, 0, size), self.ahead)
            send(s, a, k + 1, self.piece(ref, a, s, 2, 1), span(one, a, s, size, size), self.behind)
            send(s, a, k + 2, self.piece(ref, a, s, 1, 1), span(two, a, s, size, size), self.ahead)
            send(s, a, k + 3, self.piece(ref, a, s, 3, 0), span(two, a, s, 2 * size, size), self.behind)

        def total_mid(self, ref, one, two, s, a, k):
            size = self.share
            arrived(s, a, k)
            there = self.piece(ref, a, s, 1, 0)
            add_into(there, [there, span(one, a, s, 0, size)], size)
            send(s, a, k + 4, there, span(two, a, s, 0, size), self.ahead)
            arrived(s, a, k + 1)
            there = self.piece(ref, a, s, 3, 1)
            add_into(there, [there, span(one, a, s, size, size)], size)
            send(s, a, k + 5, there, span(two, a, s, 3 * size, size), self.behind)

        def addends(self, ref, two, s, a, pair):
            size = self.share
            return [
                self.piece(ref, a, s, 0, pair), span(two, a, s, pair * size, size),
                span(two, a, s, (2 + pair) * size, size),
            ]

        def total_pair(self, ref, two, outgoing, incoming, s, a, k):
            arrived(s, a, k + 2, k + 3, k + 4, k + 5)
            add_into(outgoing.at[a, s], self.addends(ref, two, s, a, 1 - self.pair), self.share)
            send(s, a, k + 6, outgoing.at[a, s], incoming.at[a, s], self.partner)

        def total_end(self, ref, two, incoming, s, a, k):
            arrived(s, a, k + 6)
            return self.addends(ref, two, s, a, self.pair) + [incoming.at[a, s]]

    def add_into(target, refs, count):
        @pl.loop(0, count // 16)
        def _(i):
            part = pl.ds(pl.multiple_of(i * 16, 16), 16)
            value = refs[0][part].astype(jnp.float32)
            for ref in refs[1:]:
                value = value + ref[part].astype(jnp.float32)
            target[part] = value.astype(target.dtype)

    row_ring = Ring(z, y_lo, ROW_SHARE, 0, z_next, z_back, y_near)
    col_ring = Ring(x, y_hi, COL_SHARE, core * (ROWS // 2), x_next, x_back, y_far)
    inputs, outputs = (tokens, cotangent), (layer_output, token_grad)

    def product(source, tile, dims, target):
        @pl.loop(0, SIDE // WIDE)
        def _(j):
            part = pl.ds(pl.multiple_of(j * WIDE, WIDE), WIDE)
            other = tiles[tile, :, part] if dims is PLAIN else tiles[tile, part, :]
            target[:, part] = lax.dot_general(
                source[...], other, dims, preferred_element_type=jnp.float32
            ).astype(jnp.bfloat16)

    def assemble(s, a):
        blocks = (widen_blocks, narrow_blocks)[a]
        spare[CAP] = jnp.zeros((BLK, BLK), jnp.bfloat16)

        @pl.loop(0, CAP)
        def _(i):
            spare[i] = blocks[0, i]

        @pl.loop(0, TILE)
        def _(i):
            for j in range(TILE):
                tiles[a, pl.ds(pl.multiple_of(i * BLK, BLK), BLK), j * BLK:(j + 1) * BLK] = spare[
                    places[a, i * TILE + j]
                ]

    def gather(s, a):
        own = col_ring.piece(gathered, a, s, 0, y_hi)
        own[...] = inputs[a][s * COL_SHARE:(s + 1) * COL_SHARE]
        col_ring.spread(gathered, s, a, COL_GATHER)

    def gather_mid(s, a):
        col_ring.spread_mid(gathered, s, a, COL_GATHER)

    def gather_pass(s, a):
        col_ring.spread_pass(gathered, s, a, COL_GATHER)

    def gather_core(s, a):
        col_ring.spread_end(s, a, COL_GATHER)
        half = span(gathered, a, s, core * (ROWS // 2), ROWS // 2)
        send(s, a, CORE_GATHER, half, half, other_core)

    def rise(s, a):
        arrived(s, a, CORE_GATHER)
        product(gathered.at[a, s], a, (PLAIN, FLIPPED)[a], terms.at[a, s])
        if (s, a) in NEAR:
            row_ring.near(terms, row_two, s, a, ROW_SUM)
        else:
            row_ring.total(terms, row_one, row_two, s, a, ROW_SUM)

    def sum_mid(s, a):
        row_ring.total_mid(terms, row_one, row_two, s, a, ROW_SUM)

    def sum_pair(s, a):
        row_ring.total_pair(terms, row_two, row_send, row_pair, s, a, ROW_SUM)

    def sumb_two(s, a):
        row_ring.near_two(terms, row_two, row_pair, s, a, ROW_SUM)

    def sumb_one(s, a):
        row_ring.near_one(terms, row_two, row_one, s, a, ROW_SUM)

    def sumb_mid(s, a):
        row_ring.near_mid(terms, row_pair, row_one, s, a, ROW_SUM)

    def sumb_end(s, a):
        bend_fields(s, a, row_ring.near_end(terms, row_two, row_one, s, a, ROW_SUM))

    def sum_end(s, a):
        bend_fields(s, a, row_ring.total_end(terms, row_two, row_pair, s, a, ROW_SUM))

    def bend_fields(s, a, refs):
        own = row_ring.piece(fields, a, s, 0, y_lo)

        @pl.loop(0, ROW_SHARE // 16)
        def _(i):
            part = pl.ds(pl.multiple_of(i * 16, 16), 16)
            value = refs[0][part].astype(jnp.float32)
            for ref in refs[1:]:
                value = value + ref[part].astype(jnp.float32)
            if a == 0:
                hidden[s, part] = value
                bend = jnp.tanh(CURVE * (value + CUBIC * (value * value * value)))
                own[part] = (0.5 * value * (1.0 + bend)).astype(jnp.bfloat16)
            else:
                at = hidden[s, part]
                square = at * at
                bend = jnp.tanh(CURVE * (at + CUBIC * (square * at)))
                slope = 0.5 * (1.0 + bend) + 0.5 * at * (1.0 - bend * bend) * CURVE * (1.0 + 3.0 * CUBIC * square)
                own[part] = (slope * value).astype(jnp.bfloat16)

        if (s, a) in WIDE_FIRST:
            row_ring.wide(fields, s, a, ROW_GATHER)
        else:
            row_ring.spread(fields, s, a, ROW_GATHER)

    def sprb_mid(s, a):
        row_ring.wide_mid(fields, s, a, ROW_GATHER)

    def sprb_pass(s, a):
        row_ring.wide_pass(fields, s, a, ROW_GATHER)

    def sprb_end(s, a):
        row_ring.wide_end(s, a, ROW_GATHER)

    def spread_mid(s, a):
        row_ring.spread_mid(fields, s, a, ROW_GATHER)

    def spread_pass(s, a):
        row_ring.spread_pass(fields, s, a, ROW_GATHER)

    def spread_end(s, a):
        row_ring.spread_end(s, a, ROW_GATHER)

    def fall(s, a):
        for k in range(ROW_SUM, ROW_GATHER):
            if (s, a, k) in copies:
                copies.pop((s, a, k)).wait_send()
        product(fields.at[a, s], 1 - a, (PLAIN, FLIPPED)[a], terms.at[a, s])
        half = span(terms, a, s, (1 - core) * (ROWS // 2), ROWS // 2)
        send(s, a, CORE_SUM, half, core_in.at[a, s], other_core)

    def core_end(s, a):
        arrived(s, a, CORE_SUM)
        half = span(terms, a, s, core * (ROWS // 2), ROWS // 2)
        add_into(half, [half, core_in.at[a, s]], ROWS // 2)
        col_ring.total(terms, col_one, col_two, s, a, COL_SUM)

    def out_mid(s, a):
        col_ring.total_mid(terms, col_one, col_two, s, a, COL_SUM)

    def out_pair(s, a):
        col_ring.total_pair(terms, col_two, col_send, col_pair, s, a, COL_SUM)

    def out_end(s, a):
        refs = col_ring.total_end(terms, col_two, col_pair, s, a, COL_SUM)
        add_into(outputs[a].at[pl.ds(s * COL_SHARE, COL_SHARE)], refs, COL_SHARE)

    def flip(s, a):
        source = gathered.at[a, s]

        @pl.loop(0, TILE)
        def _(i):
            part = pl.ds(pl.multiple_of(i * BLK, BLK), BLK)
            flipped[a, part, s * ROWS:(s + 1) * ROWS] = source[:, part].T

    def slot(j, a):
        part = pl.ds(j * WIDE, WIDE)
        right = fields[a, :, :, part].reshape(TOKENS, WIDE)

        @pl.loop(0, SIDE // WIDE)
        def _(i):
            value = lax.dot_general(
                flipped[1 - a, pl.ds(pl.multiple_of(i * WIDE, WIDE), WIDE), :], right, PLAIN,
                preferred_element_type=jnp.float32,
            )
            value = (value * (1.0 / 32.0)).astype(jnp.bfloat16)
            for r in range(WIDE // BLK):
                for c in range(WIDE // BLK):
                    place = (i * (WIDE // BLK) + r) * TILE + j * (WIDE // BLK) + c
                    dense[place] = value[r * BLK:(r + 1) * BLK, c * BLK:(c + 1) * BLK]

    def pick(s, a):
        at, target = (narrow_at, widen_at)[a], (narrow_grad, widen_grad)[a]
        dense[TILE * TILE] = jnp.zeros((BLK, BLK), jnp.bfloat16)

        @pl.loop(0, CAP // 4)
        def _(g):
            for u in range(4):
                block = dense[at[g * 4 + u]]
                target[0, g * 4 + u] = block.T if a == 0 else block

    steps = {
        step.__name__: step
        for step in (
            assemble, gather, gather_mid, gather_pass, gather_core, rise, sum_mid, sum_pair, sum_end, spread_mid,
            spread_pass, spread_end, fall, core_end, out_mid, out_pair, out_end, flip, slot, pick,
            sumb_two, sumb_one, sumb_mid, sumb_end, sprb_mid, sprb_pass, sprb_end,
        )
    }
    for index, s, a in ORDER:
        steps[STEPS[index]](s, a)
    for copy in copies.values():
        copy.wait_send()


def local(tokens, widen_blocks, widen_pattern, narrow_blocks, narrow_pattern, cotangent):
    pattern = jnp.stack([widen_pattern[0], narrow_pattern[0]])
    flat = jnp.where(pattern[..., 0] >= 0, pattern[..., 0] * TILE + pattern[..., 1], -1)
    match = flat[:, :, None] == jnp.arange(TILE * TILE, dtype=jnp.int32)
    slot = jnp.arange(CAP, dtype=jnp.int32)[None, :, None]
    places = jnp.min(jnp.where(match, slot, CAP), axis=1)
    blocks = jnp.where(pattern[..., 0] >= 0, jnp.stack([flat[0], pattern[1, :, 1] * TILE + pattern[1, :, 0]]), TILE * TILE)
    vmem, smem = pl.BlockSpec(memory_space=pltpu.VMEM), pl.BlockSpec(memory_space=pltpu.SMEM)

    def room(*shape, dtype=jnp.bfloat16):
        return pltpu.VMEM((*shape, SIDE), dtype)

    outs = pl.pallas_call(
        body,
        out_shape=(
            jax.ShapeDtypeStruct(tokens.shape, jnp.bfloat16),
            jax.ShapeDtypeStruct(tokens.shape, jnp.bfloat16),
            jax.ShapeDtypeStruct(widen_blocks.shape, jnp.bfloat16),
            jax.ShapeDtypeStruct(narrow_blocks.shape, jnp.bfloat16),
        ),
        in_specs=[smem] * 3 + [vmem] * 4,
        out_specs=[vmem] * 4,
        scratch_shapes=[
            room(2, STAGES, ROWS),
            room(2, STAGES, ROWS),
            room(2, STAGES, ROWS),
            room(2, SIDE),
            room(2, STAGES, 2 * ROW_SHARE),
            room(2, STAGES, 4 * ROW_SHARE),
            room(2, STAGES, ROW_SHARE),
            room(2, STAGES, ROW_SHARE),
            room(2, STAGES, ROWS // 2),
            room(2, STAGES, 2 * COL_SHARE),
            room(2, STAGES, 4 * COL_SHARE),
            room(2, STAGES, COL_SHARE),
            room(2, STAGES, COL_SHARE),
            room(STAGES, ROW_SHARE, dtype=jnp.float32),
            pltpu.VMEM((CAP + 1, BLK, BLK), jnp.bfloat16),
            pltpu.VMEM((2, SIDE, TOKENS), jnp.bfloat16),
            pltpu.VMEM((TILE * TILE + 1, BLK, BLK), jnp.bfloat16),
            pltpu.SemaphoreType.DMA((2, STAGES, COPIES)),
            pltpu.SemaphoreType.DMA((2, STAGES, COPIES)),
        ],
        compiler_params=pltpu.CompilerParams(
            collective_id=0, has_side_effects=True, vmem_limit_bytes=62 * 2**20
        ),
        name="layer",
    )(
        places, blocks[0], blocks[1], tokens, cotangent, widen_blocks, narrow_blocks,
    )
    return outs


def solution(mesh):
    placed = (
        P("col", "row"),
        P("row", "col", None, None),
        P("row", "col", None),
        P("row", "col", None, None),
        P("row", "col", None),
        P("col", "row"),
    )
    return jax.shard_map(
        local,
        mesh=mesh,
        in_specs=placed,
        out_specs=(
            P("col", "row"),
            P("col", "row"),
            P("row", "col", None, None),
            P("row", "col", None, None),
        ),
        check_vma=False,
    )
```

```python
import functools

import jax
import jax.numpy as jnp
from jax import lax
from jax.experimental import pallas as pl
from jax.experimental.pallas import tpu as pltpu
from jax.sharding import PartitionSpec as P

MESH = pl.DeviceIdType.MESH
BLK = 128
TILE = 12
SIDE = BLK * TILE
CAP = 36
TOKENS = 1024
STAGES = 4
ROWS = TOKENS // STAGES
ROW_SHARE = ROWS // 8
COL_SHARE = ROWS // 16
WIDE = 512
CURVE = 0.7978845608028654
CUBIC = 0.044715
PLAIN = (((1,), (0,)), ((), ()))
FLIPPED = (((1,), (1,)), ((), ()))
TALL = (((0,), (0,)), ((), ()))
COL_GATHER, CORE_GATHER, ROW_SUM, ROW_GATHER, CORE_SUM, COL_SUM, COPIES = 0, 7, 8, 18, 26, 27, 34


NEAR = ((0, 0), (0, 1), (2, 0))
WIDE_FIRST = ((0, 0), (0, 1), (1, 0))
STEPS = (
    "gather", "assemble", "gather_mid", "gather_pass", "gather_core", "rise", "sumb_two", "sum_mid", "sumb_one",
    "sumb_mid", "sum_pair", "sumb_end", "sum_end", "sprb_mid", "flip", "sprb_pass", "spread_mid", "sprb_end", "fall",
    "spread_pass", "core_end", "out_mid", "spread_end", "out_pair", "slot", "out_end", "pick",
)
ORDER = (
    (0, 0, 0), (0, 1, 0), (1, 0, 0), (0, 2, 0), (2, 0, 0), (2, 1, 0), (2, 2, 0), (0, 3, 0), (3, 0, 0), (3, 1, 0),
    (2, 3, 0), (3, 2, 0), (0, 0, 1), (1, 0, 1), (4, 0, 0), (0, 1, 1), (4, 1, 0), (3, 3, 0), (5, 0, 0), (4, 2, 0),
    (5, 1, 0), (4, 3, 0), (0, 2, 1), (0, 3, 1), (5, 2, 0), (6, 0, 0), (2, 1, 1), (7, 1, 0), (2, 0, 1), (5, 3, 0),
    (3, 0, 1), (8, 0, 0), (3, 1, 1), (9, 0, 0), (10, 1, 0), (2, 2, 1), (4, 0, 1), (7, 3, 0), (3, 2, 1), (6, 2, 0),
    (2, 3, 1), (5, 0, 1), (4, 2, 1), (8, 2, 0), (11, 0, 0), (10, 3, 0), (9, 2, 0), (5, 2, 1), (12, 1, 0), (13, 0, 0),
    (3, 3, 1), (11, 2, 0), (14, 0, 1), (6, 0, 1), (4, 3, 1), (7, 2, 1), (4, 1, 1), (14, 3, 0), (8, 0, 1), (5, 3, 1),
    (13, 1, 0), (5, 1, 1), (14, 1, 1), (12, 3, 0), (9, 0, 1), (14, 1, 0), (10, 2, 1), (14, 3, 1), (14, 0, 0),
    (14, 2, 0), (14, 2, 1), (7, 3, 1), (15, 0, 0), (16, 2, 0), (15, 1, 0), (7, 1, 1), (16, 3, 0), (11, 0, 1),
    (12, 2, 1), (10, 3, 1), (17, 0, 0), (18, 0, 0), (19, 2, 0), (17, 1, 0), (18, 1, 0), (10, 1, 1), (20, 0, 0),
    (19, 3, 0), (16, 2, 1), (20, 1, 0), (21, 0, 0), (12, 3, 1), (13, 0, 1), (21, 1, 0), (12, 1, 1), (22, 2, 0),
    (18, 2, 0), (23, 0, 0), (22, 3, 0), (18, 3, 0), (19, 2, 1), (20, 2, 0), (16, 3, 1), (24, 0, 0), (20, 3, 0),
    (15, 0, 1), (21, 2, 0), (16, 1, 1), (25, 0, 0), (23, 1, 0), (24, 1, 0), (22, 2, 1), (18, 2, 1), (23, 2, 0),
    (17, 0, 1), (18, 0, 1), (19, 1, 1), (19, 3, 1), (20, 2, 1), (21, 3, 0), (24, 2, 0), (20, 0, 1), (21, 2, 1),
    (22, 1, 1), (18, 1, 1), (22, 3, 1), (18, 3, 1), (21, 0, 1), (23, 3, 0), (20, 1, 1), (23, 2, 1), (26, 0, 0),
    (20, 3, 1), (24, 0, 1), (25, 3, 0), (21, 1, 1), (21, 3, 1), (25, 1, 0), (23, 0, 1), (24, 1, 1), (23, 1, 1),
    (23, 3, 1), (24, 2, 1), (25, 0, 1), (25, 2, 0), (25, 2, 1), (25, 1, 1), (26, 0, 1), (25, 3, 1),
)


def body(
    widen_at, narrow_at, tokens, cotangent, widen_blocks, narrow_blocks,
    layer_output, token_grad, widen_grad, narrow_grad,
    gathered, terms, fields, tiles, row_one, row_two, row_pair, row_send, core_in,
    col_one, col_two, col_pair, col_send, hidden, widen_spare, narrow_spare, flipped, dense, picked, results, at, marks, places,
    send_sem, recv_sem, here_sem,
):
    row, col = lax.axis_index("row"), lax.axis_index("col")
    y_lo, z = row // 4, row % 4
    x, y_hi, core = col // 4, (col // 2) % 2, col % 2

    def on_row(pair, ring):
        return (pair * 4 + ring % 4, col)

    def on_col(ring, pair, side):
        return (row, (ring % 4) * 4 + pair * 2 + side)

    z_next, z_back, y_near = on_row(y_lo, z + 1), on_row(y_lo, z + 3), on_row(1 - y_lo, z)
    x_next, x_back = on_col(x + 1, y_hi, core), on_col(x + 3, y_hi, core)
    y_far, other_core = on_col(x, 1 - y_hi, core), on_col(x, y_hi, 1 - core)

    spare = (widen_spare, narrow_spare)
    own_rows = pl.multiple_of(core * (ROWS // 2) + (x * 2 + y_hi) * COL_SHARE, COL_SHARE)
    loads = {}
    for i, (source, target) in enumerate((
        (tokens, gathered.at[0, :, pl.ds(own_rows, COL_SHARE)]),
        (widen_at, at.at[0]),
        (narrow_at, at.at[1]),
        (cotangent, gathered.at[1, :, pl.ds(own_rows, COL_SHARE)]),
        (widen_blocks.at[0], widen_spare.at[pl.ds(0, CAP)]),
        (narrow_blocks.at[0], narrow_spare.at[pl.ds(0, CAP)]),
    )):
        loads[i] = pltpu.make_async_copy(source, target, here_sem.at[i])
        loads[i].start()

    barrier = pltpu.get_barrier_semaphore()
    partners = (z_next, z_back, y_near, x_next, x_back, y_far, other_core)
    for partner in partners:
        pl.semaphore_signal(barrier, inc=1, device_id=partner, device_id_type=MESH)

    def place(a, i):
        return (at[a, 0, i] + 1) * TILE + at[a, 1, i] + 1

    count = lax.broadcasted_iota(jnp.int32, (1, 2 * BLK), 1)
    for a in range(2):
        loads[1 + a].wait()
        marks[a:a + 1] = lax.fori_loop(
            0, CAP, lambda i, mark: jnp.where(count == place(a, i), i, mark), jnp.full((1, 2 * BLK), CAP, jnp.int32)
        )
    loads[6] = pltpu.make_async_copy(marks, places, here_sem.at[6])
    loads[6].start()
    for a in range(2):
        spare[a][CAP] = jnp.zeros((BLK, BLK), jnp.bfloat16)
    dense[0] = jnp.zeros((BLK, BLK), jnp.bfloat16)
    loads[6].wait()
    pl.semaphore_wait(barrier, len(partners))

    copies = {}

    def send(s, a, k, source, target, device):
        copy = pltpu.make_async_remote_copy(
            src_ref=source, dst_ref=target, send_sem=send_sem.at[a, s, k], recv_sem=recv_sem.at[a, s, k],
            device_id=device, device_id_type=MESH,
        )
        copy.start()
        copies[s, a, k] = copy

    def arrived(s, a, *ks):
        for k in ks:
            copies[s, a, k].wait_recv()

    def span(ref, a, s, start, length):
        return ref.at[a, s, pl.ds(pl.multiple_of(start, length), length)]

    class Ring:
        def __init__(self, place, pair, share, base, ahead, behind, partner):
            self.place, self.pair, self.share, self.base = place, pair, share, base
            self.ahead, self.behind, self.partner = ahead, behind, partner

        def piece(self, ref, a, s, step, pair):
            return span(ref, a, s, self.base + (((self.place + step) % 4) * 2 + pair) * self.share, self.share)

        def spread(self, ref, s, a, k):
            own = self.piece(ref, a, s, 0, self.pair)
            send(s, a, k, own, own, self.partner)
            send(s, a, k + 1, own, own, self.ahead)
            send(s, a, k + 2, own, own, self.behind)

        def spread_mid(self, ref, s, a, k):
            arrived(s, a, k)
            near = self.piece(ref, a, s, 0, 1 - self.pair)
            send(s, a, k + 3, near, near, self.ahead)
            send(s, a, k + 4, near, near, self.behind)

        def spread_pass(self, ref, s, a, k):
            arrived(s, a, k + 1)
            left = self.piece(ref, a, s, 3, self.pair)
            send(s, a, k + 5, left, left, self.ahead)
            arrived(s, a, k + 4)
            right = self.piece(ref, a, s, 1, 1 - self.pair)
            send(s, a, k + 6, right, right, self.behind)

        def spread_end(self, s, a, k):
            arrived(s, a, k + 2, k + 3, k + 5, k + 6)

        def half(self, ref, which):
            size = self.share // 2
            return ref.at[pl.ds(which * size, size)]

        def wide(self, ref, s, a, k):
            own = self.piece(ref, a, s, 0, self.pair)
            send(s, a, k, own, own, self.ahead)
            send(s, a, k + 1, own, own, self.behind)
            send(s, a, k + 4, own, own, self.partner)

        def wide_mid(self, ref, s, a, k):
            left, right = self.piece(ref, a, s, 3, self.pair), self.piece(ref, a, s, 1, self.pair)
            arrived(s, a, k)
            send(s, a, k + 2, self.half(left, 0), self.half(left, 0), self.ahead)
            arrived(s, a, k + 1)
            send(s, a, k + 3, self.half(right, 1), self.half(right, 1), self.behind)
            send(s, a, k + 5, left, left, self.partner)
            send(s, a, k + 6, right, right, self.partner)

        def wide_pass(self, ref, s, a, k):
            arrived(s, a, k + 2, k + 3)
            far = self.piece(ref, a, s, 2, self.pair)
            send(s, a, k + 7, far, far, self.partner)

        def wide_end(self, s, a, k):
            arrived(s, a, k + 4, k + 5, k + 6, k + 7)

        def near(self, ref, near, s, a, k):
            for i, step in enumerate((2, 1, 3, 0)):
                source = self.piece(ref, a, s, step, 1 - self.pair)
                send(s, a, k + i, source, span(near, a, s, step * self.share, self.share), self.partner)

        def join(self, ref, near, s, a, step):
            there = self.piece(ref, a, s, step, self.pair)
            add_into(there, [there, span(near, a, s, step * self.share, self.share)], self.share)
            return there

        def near_two(self, ref, near, one, s, a, k):
            arrived(s, a, k)
            there = self.join(ref, near, s, a, 2)
            send(s, a, k + 4, self.half(there, 0), self.half(one.at[a, s], 0), self.ahead)
            send(s, a, k + 5, self.half(there, 1), self.half(one.at[a, s], 1), self.behind)

        def near_one(self, ref, near, two, s, a, k):
            size = self.share
            arrived(s, a, k + 1)
            there = self.join(ref, near, s, a, 1)
            send(s, a, k + 6, self.half(there, 1), self.half(span(two, a, s, 0, size), 1), self.ahead)
            arrived(s, a, k + 2)
            there = self.join(ref, near, s, a, 3)
            send(s, a, k + 7, self.half(there, 0), self.half(span(two, a, s, size, size), 0), self.behind)

        def near_mid(self, ref, one, two, s, a, k):
            size = self.share
            arrived(s, a, k + 4)
            there = self.half(self.piece(ref, a, s, 1, self.pair), 0)
            add_into(there, [there, self.half(one.at[a, s], 0)], size // 2)
            send(s, a, k + 8, there, self.half(span(two, a, s, 0, size), 0), self.ahead)
            arrived(s, a, k + 5)
            there = self.half(self.piece(ref, a, s, 3, self.pair), 1)
            add_into(there, [there, self.half(one.at[a, s], 1)], size // 2)
            send(s, a, k + 9, there, self.half(span(two, a, s, size, size), 1), self.behind)

        def near_end(self, ref, near, two, s, a, k):
            size = self.share
            arrived(s, a, k + 3, k + 6, k + 7, k + 8, k + 9)
            return [
                self.piece(ref, a, s, 0, self.pair), span(near, a, s, 0, size),
                span(two, a, s, 0, size), span(two, a, s, size, size),
            ]

        def total(self, ref, one, two, s, a, k):
            size = self.share
            send(s, a, k, self.piece(ref, a, s, 2, 0), span(one, a, s, 0, size), self.ahead)
            send(s, a, k + 1, self.piece(ref, a, s, 2, 1), span(one, a, s, size, size), self.behind)
            send(s, a, k + 2, self.piece(ref, a, s, 1, 1), span(two, a, s, size, size), self.ahead)
            send(s, a, k + 3, self.piece(ref, a, s, 3, 0), span(two, a, s, 2 * size, size), self.behind)

        def total_mid(self, ref, one, two, s, a, k):
            size = self.share
            arrived(s, a, k)
            there = self.piece(ref, a, s, 1, 0)
            add_into(there, [there, span(one, a, s, 0, size)], size)
            send(s, a, k + 4, there, span(two, a, s, 0, size), self.ahead)
            arrived(s, a, k + 1)
            there = self.piece(ref, a, s, 3, 1)
            add_into(there, [there, span(one, a, s, size, size)], size)
            send(s, a, k + 5, there, span(two, a, s, 3 * size, size), self.behind)

        def addends(self, ref, two, s, a, pair):
            size = self.share
            return [
                self.piece(ref, a, s, 0, pair), span(two, a, s, pair * size, size),
                span(two, a, s, (2 + pair) * size, size),
            ]

        def total_pair(self, ref, two, outgoing, incoming, s, a, k):
            arrived(s, a, k + 2, k + 3, k + 4, k + 5)
            add_into(outgoing.at[a, s], self.addends(ref, two, s, a, 1 - self.pair), self.share)
            send(s, a, k + 6, outgoing.at[a, s], incoming.at[a, s], self.partner)

        def total_end(self, ref, two, incoming, s, a, k):
            arrived(s, a, k + 6)
            return self.addends(ref, two, s, a, self.pair) + [incoming.at[a, s]]

    def add_into(target, refs, count):
        @pl.loop(0, count // 16)
        def _(i):
            part = pl.ds(pl.multiple_of(i * 16, 16), 16)
            value = refs[0][part].astype(jnp.float32)
            for ref in refs[1:]:
                value = value + ref[part].astype(jnp.float32)
            target[part] = value.astype(target.dtype)

    row_ring = Ring(z, y_lo, ROW_SHARE, 0, z_next, z_back, y_near)
    col_ring = Ring(x, y_hi, COL_SHARE, core * (ROWS // 2), x_next, x_back, y_far)
    outputs, stores = (layer_output, token_grad), []

    def product(source, tile, dims, target):
        @pl.loop(0, SIDE // WIDE)
        def _(j):
            part = pl.ds(pl.multiple_of(j * WIDE, WIDE), WIDE)
            other = tiles[tile, :, part] if dims is PLAIN else tiles[tile, part, :]
            target[:, part] = lax.dot_general(
                source[...], other, dims, preferred_element_type=jnp.float32
            ).astype(jnp.bfloat16)

    def assemble(s, a):
        loads[4 + a].wait()

        @pl.loop(0, TILE)
        def _(i):
            for j in range(TILE):
                tiles[a, pl.ds(pl.multiple_of(i * BLK, BLK), BLK), j * BLK:(j + 1) * BLK] = spare[a][
                    places[a, (i + 1) * TILE + j + 1]
                ]

    def gather(s, a):
        if s == 0:
            loads[3 * a].wait()
        col_ring.spread(gathered, s, a, COL_GATHER)

    def gather_mid(s, a):
        col_ring.spread_mid(gathered, s, a, COL_GATHER)

    def gather_pass(s, a):
        col_ring.spread_pass(gathered, s, a, COL_GATHER)

    def gather_core(s, a):
        col_ring.spread_end(s, a, COL_GATHER)
        half = span(gathered, a, s, core * (ROWS // 2), ROWS // 2)
        send(s, a, CORE_GATHER, half, half, other_core)

    def rise(s, a):
        arrived(s, a, CORE_GATHER)
        product(gathered.at[a, s], a, (PLAIN, FLIPPED)[a], terms.at[a, s])
        if (s, a) in NEAR:
            row_ring.near(terms, row_two, s, a, ROW_SUM)
        else:
            row_ring.total(terms, row_one, row_two, s, a, ROW_SUM)

    def sum_mid(s, a):
        row_ring.total_mid(terms, row_one, row_two, s, a, ROW_SUM)

    def sum_pair(s, a):
        row_ring.total_pair(terms, row_two, row_send, row_pair, s, a, ROW_SUM)

    def sumb_two(s, a):
        row_ring.near_two(terms, row_two, row_pair, s, a, ROW_SUM)

    def sumb_one(s, a):
        row_ring.near_one(terms, row_two, row_one, s, a, ROW_SUM)

    def sumb_mid(s, a):
        row_ring.near_mid(terms, row_pair, row_one, s, a, ROW_SUM)

    def sumb_end(s, a):
        bend_fields(s, a, row_ring.near_end(terms, row_two, row_one, s, a, ROW_SUM))

    def sum_end(s, a):
        bend_fields(s, a, row_ring.total_end(terms, row_two, row_pair, s, a, ROW_SUM))

    def bend_fields(s, a, refs):
        own = row_ring.piece(fields, a, s, 0, y_lo)

        @pl.loop(0, ROW_SHARE // 16)
        def _(i):
            part = pl.ds(pl.multiple_of(i * 16, 16), 16)
            value = refs[0][part].astype(jnp.float32)
            for ref in refs[1:]:
                value = value + ref[part].astype(jnp.float32)
            if a == 0:
                hidden[s, part] = value
                bend = jnp.tanh(CURVE * (value + CUBIC * (value * value * value)))
                own[part] = (0.5 * value * (1.0 + bend)).astype(jnp.bfloat16)
            else:
                at = hidden[s, part]
                square = at * at
                bend = jnp.tanh(CURVE * (at + CUBIC * (square * at)))
                slope = 0.5 * (1.0 + bend) + 0.5 * at * (1.0 - bend * bend) * CURVE * (1.0 + 3.0 * CUBIC * square)
                own[part] = (slope * value).astype(jnp.bfloat16)

        if (s, a) in WIDE_FIRST:
            row_ring.wide(fields, s, a, ROW_GATHER)
        else:
            row_ring.spread(fields, s, a, ROW_GATHER)

    def sprb_mid(s, a):
        row_ring.wide_mid(fields, s, a, ROW_GATHER)

    def sprb_pass(s, a):
        row_ring.wide_pass(fields, s, a, ROW_GATHER)

    def sprb_end(s, a):
        row_ring.wide_end(s, a, ROW_GATHER)

    def spread_mid(s, a):
        row_ring.spread_mid(fields, s, a, ROW_GATHER)

    def spread_pass(s, a):
        row_ring.spread_pass(fields, s, a, ROW_GATHER)

    def spread_end(s, a):
        row_ring.spread_end(s, a, ROW_GATHER)

    def fall(s, a):
        for k in range(ROW_SUM, ROW_GATHER):
            if (s, a, k) in copies:
                copies.pop((s, a, k)).wait_send()
        product(fields.at[a, s], 1 - a, (PLAIN, FLIPPED)[a], terms.at[a, s])
        half = span(terms, a, s, (1 - core) * (ROWS // 2), ROWS // 2)
        send(s, a, CORE_SUM, half, core_in.at[a, s], other_core)

    def core_end(s, a):
        arrived(s, a, CORE_SUM)
        half = span(terms, a, s, core * (ROWS // 2), ROWS // 2)
        add_into(half, [half, core_in.at[a, s]], ROWS // 2)
        col_ring.total(terms, col_one, col_two, s, a, COL_SUM)

    def out_mid(s, a):
        col_ring.total_mid(terms, col_one, col_two, s, a, COL_SUM)

    def out_pair(s, a):
        col_ring.total_pair(terms, col_two, col_send, col_pair, s, a, COL_SUM)

    def out_end(s, a):
        refs = col_ring.total_end(terms, col_two, col_pair, s, a, COL_SUM)
        add_into(results.at[a, s], refs, COL_SHARE)
        store = pltpu.make_async_copy(results.at[a, s], outputs[a].at[s], here_sem.at[9 + a * STAGES + s])
        store.start()
        stores.append(store)

    def flip(s, a):
        source = gathered.at[a, s]

        @pl.loop(0, TILE)
        def _(i):
            part = pl.ds(pl.multiple_of(i * BLK, BLK), BLK)
            flipped[a, part, s * ROWS:(s + 1) * ROWS] = source[:, part].T

    def slot(j, a):
        part = pl.ds(j * WIDE, WIDE)
        right = fields[a, :, :, part].reshape(TOKENS, WIDE)

        @pl.loop(0, SIDE // WIDE)
        def _(i):
            value = lax.dot_general(
                flipped[1 - a, pl.ds(pl.multiple_of(i * WIDE, WIDE), WIDE), :], right, PLAIN,
                preferred_element_type=jnp.float32,
            )
            value = (value * (1.0 / 32.0)).astype(jnp.bfloat16)
            for r in range(WIDE // BLK):
                for c in range(WIDE // BLK):
                    spot = (i * (WIDE // BLK) + r + 1) * TILE + j * (WIDE // BLK) + c + 1
                    dense[spot] = value[r * BLK:(r + 1) * BLK, c * BLK:(c + 1) * BLK]

    def pick(s, a):
        target = (narrow_grad, widen_grad)[a]

        @pl.loop(0, CAP // 4)
        def _(g):
            for u in range(4):
                i = g * 4 + u
                if a == 0:
                    row_at, col_at = at[1, 0, i], at[1, 1, i]
                    picked[a, i] = dense[(col_at + 1) * TILE + row_at + 1].T
                else:
                    picked[a, i] = dense[place(0, i)]

        store = pltpu.make_async_copy(picked.at[a], target.at[0], here_sem.at[7 + a])
        store.start()
        stores.append(store)

    steps = {
        step.__name__: step
        for step in (
            assemble, gather, gather_mid, gather_pass, gather_core, rise, sum_mid, sum_pair, sum_end, spread_mid,
            spread_pass, spread_end, fall, core_end, out_mid, out_pair, out_end, flip, slot, pick,
            sumb_two, sumb_one, sumb_mid, sumb_end, sprb_mid, sprb_pass, sprb_end,
        )
    }
    for index, s, a in ORDER:
        steps[STEPS[index]](s, a)
    for copy in copies.values():
        copy.wait_send()
    for store in stores:
        store.wait()


def hand_on(*refs):
    sources, targets, rooms, sem = refs[:4], refs[4:8], refs[8:12], refs[12]
    loads = [pltpu.make_async_copy(a, b, sem.at[0, i]) for i, (a, b) in enumerate(zip(sources, rooms))]
    stores = [pltpu.make_async_copy(a, b, sem.at[1, i]) for i, (a, b) in enumerate(zip(rooms, targets))]
    for load in loads:
        load.start()
    for load, store in zip(loads, stores):
        load.wait()
        store.start()
    for store in stores:
        store.wait()


def local(tokens, widen_blocks, widen_pattern, narrow_blocks, narrow_pattern, cotangent):
    grouped = (STAGES, COL_SHARE, SIDE)
    anywhere = pl.BlockSpec(memory_space=pl.ANY)
    results = (
        jax.ShapeDtypeStruct(grouped, jnp.bfloat16),
        jax.ShapeDtypeStruct(grouped, jnp.bfloat16),
        jax.ShapeDtypeStruct(widen_blocks.shape, jnp.bfloat16),
        jax.ShapeDtypeStruct(narrow_blocks.shape, jnp.bfloat16),
    )

    def room(*shape, dtype=jnp.bfloat16):
        return pltpu.VMEM((*shape, SIDE), dtype)

    outs = pl.pallas_call(
        body,
        out_shape=results,
        in_specs=[anywhere] * 6,
        out_specs=[anywhere] * 4,
        scratch_shapes=[
            room(2, STAGES, ROWS),
            room(2, STAGES, ROWS),
            room(2, STAGES, ROWS),
            room(2, SIDE),
            room(2, STAGES, 2 * ROW_SHARE),
            room(2, STAGES, 4 * ROW_SHARE),
            room(2, STAGES, ROW_SHARE),
            room(2, STAGES, ROW_SHARE),
            room(2, STAGES, ROWS // 2),
            room(2, STAGES, 2 * COL_SHARE),
            room(2, STAGES, 4 * COL_SHARE),
            room(2, STAGES, COL_SHARE),
            room(2, STAGES, COL_SHARE),
            room(STAGES, ROW_SHARE, dtype=jnp.float32),
            pltpu.VMEM((CAP + 1, BLK, BLK), jnp.bfloat16),
            pltpu.VMEM((CAP + 1, BLK, BLK), jnp.bfloat16),
            pltpu.VMEM((2, SIDE, TOKENS), jnp.bfloat16),
            pltpu.VMEM((TILE * (TILE + 1) + 1, BLK, BLK), jnp.bfloat16),
            pltpu.VMEM((2, CAP, BLK, BLK), jnp.bfloat16),
            pltpu.VMEM((2, *grouped), jnp.bfloat16),
            pltpu.SMEM((2, 2, CAP), jnp.int32),
            pltpu.VMEM((2, 2 * BLK), jnp.int32),
            pltpu.SMEM((2, 2 * BLK), jnp.int32),
            pltpu.SemaphoreType.DMA((2, STAGES, COPIES)),
            pltpu.SemaphoreType.DMA((2, STAGES, COPIES)),
            pltpu.SemaphoreType.DMA((9 + 2 * STAGES,)),
        ],
        compiler_params=pltpu.CompilerParams(
            collective_id=0, has_side_effects=True, vmem_limit_bytes=62 * 2**20
        ),
        name="layer",
    )(
        widen_pattern[0].T, narrow_pattern[0].T, tokens.reshape(grouped), cotangent.reshape(grouped),
        widen_blocks, narrow_blocks,
    )
    outs = pl.pallas_call(
        hand_on, out_shape=results, in_specs=[anywhere] * 4, out_specs=[anywhere] * 4,
        scratch_shapes=[pltpu.VMEM(r.shape, r.dtype) for r in results] + [pltpu.SemaphoreType.DMA((2, 4))],
        name="hand_on",
    )(*outs)
    return outs[0].reshape(tokens.shape), outs[1].reshape(tokens.shape), outs[2], outs[3]


def solution(mesh):
    placed = (
        P("col", "row"),
        P("row", "col", None, None),
        P("row", "col", None),
        P("row", "col", None, None),
        P("row", "col", None),
        P("col", "row"),
    )
    return jax.shard_map(
        local,
        mesh=mesh,
        in_specs=placed,
        out_specs=(
            P("col", "row"),
            P("col", "row"),
            P("row", "col", None, None),
            P("row", "col", None, None),
        ),
        check_vma=False,
    )
```

```python
import functools

import jax
import jax.numpy as jnp
from jax import lax
from jax.experimental import pallas as pl
from jax.experimental.pallas import tpu as pltpu
from jax.sharding import PartitionSpec as P

MESH = pl.DeviceIdType.MESH
BLK = 128
TILE = 12
SIDE = BLK * TILE
CAP = 36
SLOTS = 12
TOKENS = 1024
STAGES = 4
ROWS = TOKENS // STAGES
ROW_SHARE = ROWS // 8
COL_SHARE = ROWS // 16
WIDE = 768
CURVE = 0.7978845608028654
CUBIC = 0.044715
PLAIN = (((1,), (0,)), ((), ()))
FLIPPED = (((1,), (1,)), ((), ()))
TALL = (((0,), (0,)), ((), ()))
COL_GATHER, CORE_GATHER, ROW_SUM, ROW_GATHER, CORE_SUM, COL_SUM, COPIES = 0, 7, 8, 18, 26, 27, 34


NEAR = ((1, 0), (1, 1), (3, 0))
WIDE_FIRST = ((0, 1), (1, 0), (2, 0))
STEPS = (
    "gather", "assemble", "gather_mid", "gather_pass", "gather_core", "rise", "sum_mid", "sum_pair", "sumb_two",
    "sumb_one", "sum_end", "sumb_mid", "sumb_end", "spread_mid", "sprb_mid", "sprb_pass", "spread_pass", "flip",
    "sprb_end", "fall", "spread_end", "core_end", "out_mid", "out_pair", "slot", "out_end",
)
ORDER = (
    (0, 0, 0), (0, 1, 0), (1, 0, 0), (0, 2, 0), (2, 0, 0), (2, 1, 0), (2, 2, 0), (3, 0, 0), (3, 1, 0), (3, 2, 0),
    (4, 0, 0), (0, 3, 0), (0, 0, 1), (1, 0, 1), (0, 3, 1), (0, 2, 1), (4, 1, 0), (5, 0, 0), (2, 3, 0), (4, 2, 0),
    (2, 0, 1), (0, 1, 1), (5, 1, 0), (3, 3, 0), (6, 0, 0), (2, 1, 1), (3, 0, 1), (5, 2, 0), (4, 3, 0), (2, 2, 1),
    (3, 1, 1), (7, 0, 0), (5, 3, 0), (4, 0, 1), (8, 1, 0), (9, 1, 0), (4, 1, 1), (6, 2, 0), (5, 0, 1), (7, 2, 0),
    (2, 3, 1), (10, 0, 0), (11, 1, 0), (8, 3, 0), (6, 0, 1), (3, 3, 1), (5, 1, 1), (3, 2, 1), (12, 1, 0), (9, 3, 0),
    (10, 2, 0), (13, 0, 0), (4, 2, 1), (5, 2, 1), (14, 1, 0), (8, 1, 1), (7, 0, 1), (9, 1, 1), (15, 1, 0), (16, 0, 0),
    (14, 2, 0), (6, 2, 1), (11, 1, 1), (11, 3, 0), (4, 3, 1), (5, 3, 1), (12, 3, 0), (15, 2, 0), (17, 0, 1),
    (18, 1, 0), (19, 1, 0), (7, 2, 1), (10, 0, 1), (6, 3, 1), (13, 3, 0), (12, 1, 1), (18, 2, 0), (19, 2, 0),
    (17, 1, 1), (14, 0, 1), (17, 3, 0), (20, 0, 0), (19, 0, 0), (10, 2, 1), (16, 3, 0), (7, 3, 1), (21, 2, 0),
    (17, 3, 1), (21, 1, 0), (13, 1, 1), (15, 0, 1), (17, 0, 0), (13, 2, 1), (20, 3, 0), (19, 3, 0), (22, 2, 0),
    (10, 3, 1), (22, 1, 0), (21, 0, 0), (16, 1, 1), (18, 0, 1), (19, 0, 1), (21, 3, 0), (13, 3, 1), (17, 2, 1),
    (21, 0, 1), (16, 2, 1), (20, 1, 1), (19, 1, 1), (23, 2, 0), (22, 0, 0), (22, 3, 0), (16, 3, 1), (24, 2, 0),
    (22, 0, 1), (20, 2, 1), (19, 2, 1), (21, 1, 1), (23, 0, 0), (20, 3, 1), (19, 3, 1), (21, 2, 1), (22, 1, 1),
    (23, 0, 1), (23, 1, 0), (17, 1, 0), (23, 3, 0), (21, 3, 1), (24, 1, 0), (17, 2, 0), (22, 2, 1), (23, 1, 1),
    (24, 2, 1), (22, 3, 1), (24, 0, 1), (25, 0, 0), (25, 3, 0), (25, 1, 1), (25, 2, 0), (23, 2, 1), (23, 3, 1),
    (25, 1, 0), (24, 1, 1), (25, 0, 1), (24, 0, 0), (25, 2, 1), (25, 3, 1),
)


def body(
    widen_at, narrow_at, tokens, cotangent, widen_blocks, narrow_blocks,
    layer_output, token_grad, widen_grad, narrow_grad,
    gathered, terms, fields, tiles, row_one, row_two, row_pair, row_send, core_in,
    col_one, col_two, col_pair, col_send, hidden, widen_spare, narrow_spare, flipped, blocked, at, marks, places,
    send_sem, recv_sem, here_sem,
):
    row, col = lax.axis_index("row"), lax.axis_index("col")
    y_lo, z = row // 4, row % 4
    x, y_hi, core = col // 4, (col // 2) % 2, col % 2

    def on_row(pair, ring):
        return (pair * 4 + ring % 4, col)

    def on_col(ring, pair, side):
        return (row, (ring % 4) * 4 + pair * 2 + side)

    z_next, z_back, y_near = on_row(y_lo, z + 1), on_row(y_lo, z + 3), on_row(1 - y_lo, z)
    x_next, x_back = on_col(x + 1, y_hi, core), on_col(x + 3, y_hi, core)
    y_far, other_core = on_col(x, 1 - y_hi, core), on_col(x, y_hi, 1 - core)

    spare = (widen_spare, narrow_spare)
    own_rows = pl.multiple_of(core * (ROWS // 2) + (x * 2 + y_hi) * COL_SHARE, COL_SHARE)
    loads = {}
    for i, (source, target) in enumerate((
        (tokens, gathered.at[0, :, pl.ds(own_rows, COL_SHARE)]),
        (widen_at, at.at[0]),
        (narrow_at, at.at[1]),
        (cotangent, gathered.at[1, :, pl.ds(own_rows, COL_SHARE)]),
        (widen_blocks.at[0], widen_spare.at[pl.ds(0, CAP)]),
        (narrow_blocks.at[0], narrow_spare.at[pl.ds(0, CAP)]),
    )):
        loads[i] = pltpu.make_async_copy(source, target, here_sem.at[i])
        loads[i].start()

    barrier = pltpu.get_barrier_semaphore()
    partners = (z_next, z_back, y_near, x_next, x_back, y_far, other_core)
    for partner in partners:
        pl.semaphore_signal(barrier, inc=1, device_id=partner, device_id_type=MESH)

    for a in range(2):
        spare[a][CAP] = jnp.zeros((BLK, BLK), jnp.bfloat16)
        flipped[a, 0] = jnp.zeros((BLK, TOKENS), jnp.bfloat16)
        blocked[a, :, 0] = jnp.zeros((STAGES, ROWS, BLK), jnp.bfloat16)
    pl.semaphore_wait(barrier, len(partners))

    copies = {}

    def send(s, a, k, source, target, device):
        copy = pltpu.make_async_remote_copy(
            src_ref=source, dst_ref=target, send_sem=send_sem.at[a, s, k], recv_sem=recv_sem.at[a, s, k],
            device_id=device, device_id_type=MESH,
        )
        copy.start()
        copies[s, a, k] = copy

    def arrived(s, a, *ks):
        for k in ks:
            copies[s, a, k].wait_recv()

    def span(ref, a, s, start, length):
        return ref.at[a, s, pl.ds(pl.multiple_of(start, length), length)]

    class Ring:
        def __init__(self, place, pair, share, base, ahead, behind, partner):
            self.place, self.pair, self.share, self.base = place, pair, share, base
            self.ahead, self.behind, self.partner = ahead, behind, partner

        def piece(self, ref, a, s, step, pair):
            return span(ref, a, s, self.base + (((self.place + step) % 4) * 2 + pair) * self.share, self.share)

        def spread(self, ref, s, a, k):
            own = self.piece(ref, a, s, 0, self.pair)
            send(s, a, k, own, own, self.partner)
            send(s, a, k + 1, own, own, self.ahead)
            send(s, a, k + 2, own, own, self.behind)

        def spread_mid(self, ref, s, a, k):
            arrived(s, a, k)
            near = self.piece(ref, a, s, 0, 1 - self.pair)
            send(s, a, k + 3, near, near, self.ahead)
            send(s, a, k + 4, near, near, self.behind)

        def spread_pass(self, ref, s, a, k):
            arrived(s, a, k + 1)
            left = self.piece(ref, a, s, 3, self.pair)
            send(s, a, k + 5, left, left, self.ahead)
            arrived(s, a, k + 4)
            right = self.piece(ref, a, s, 1, 1 - self.pair)
            send(s, a, k + 6, right, right, self.behind)

        def spread_end(self, s, a, k):
            arrived(s, a, k + 2, k + 3, k + 5, k + 6)

        def half(self, ref, which):
            size = self.share // 2
            return ref.at[pl.ds(which * size, size)]

        def wide(self, ref, s, a, k):
            own = self.piece(ref, a, s, 0, self.pair)
            send(s, a, k, own, own, self.ahead)
            send(s, a, k + 1, own, own, self.behind)
            send(s, a, k + 4, own, own, self.partner)

        def wide_mid(self, ref, s, a, k):
            left, right = self.piece(ref, a, s, 3, self.pair), self.piece(ref, a, s, 1, self.pair)
            arrived(s, a, k)
            send(s, a, k + 2, self.half(left, 0), self.half(left, 0), self.ahead)
            arrived(s, a, k + 1)
            send(s, a, k + 3, self.half(right, 1), self.half(right, 1), self.behind)
            send(s, a, k + 5, left, left, self.partner)
            send(s, a, k + 6, right, right, self.partner)

        def wide_pass(self, ref, s, a, k):
            arrived(s, a, k + 2, k + 3)
            far = self.piece(ref, a, s, 2, self.pair)
            send(s, a, k + 7, far, far, self.partner)

        def wide_end(self, s, a, k):
            arrived(s, a, k + 4, k + 5, k + 6, k + 7)

        def near(self, ref, near, s, a, k):
            for i, step in enumerate((2, 1, 3, 0)):
                source = self.piece(ref, a, s, step, 1 - self.pair)
                send(s, a, k + i, source, span(near, a, s, step * self.share, self.share), self.partner)

        def join(self, ref, near, s, a, step):
            there = self.piece(ref, a, s, step, self.pair)
            add_into(there, [there, span(near, a, s, step * self.share, self.share)], self.share)
            return there

        def near_two(self, ref, near, one, s, a, k):
            arrived(s, a, k)
            there = self.join(ref, near, s, a, 2)
            send(s, a, k + 4, self.half(there, 0), self.half(one.at[a, s], 0), self.ahead)
            send(s, a, k + 5, self.half(there, 1), self.half(one.at[a, s], 1), self.behind)

        def near_one(self, ref, near, two, s, a, k):
            size = self.share
            arrived(s, a, k + 1)
            there = self.join(ref, near, s, a, 1)
            send(s, a, k + 6, self.half(there, 1), self.half(span(two, a, s, 0, size), 1), self.ahead)
            arrived(s, a, k + 2)
            there = self.join(ref, near, s, a, 3)
            send(s, a, k + 7, self.half(there, 0), self.half(span(two, a, s, size, size), 0), self.behind)

        def near_mid(self, ref, one, two, s, a, k):
            size = self.share
            arrived(s, a, k + 4)
            there = self.half(self.piece(ref, a, s, 1, self.pair), 0)
            add_into(there, [there, self.half(one.at[a, s], 0)], size // 2)
            send(s, a, k + 8, there, self.half(span(two, a, s, 0, size), 0), self.ahead)
            arrived(s, a, k + 5)
            there = self.half(self.piece(ref, a, s, 3, self.pair), 1)
            add_into(there, [there, self.half(one.at[a, s], 1)], size // 2)
            send(s, a, k + 9, there, self.half(span(two, a, s, size, size), 1), self.behind)

        def near_end(self, ref, near, two, s, a, k):
            size = self.share
            arrived(s, a, k + 3, k + 6, k + 7, k + 8, k + 9)
            return [
                self.piece(ref, a, s, 0, self.pair), span(near, a, s, 0, size),
                span(two, a, s, 0, size), span(two, a, s, size, size),
            ]

        def total(self, ref, one, two, s, a, k):
            size = self.share
            send(s, a, k, self.piece(ref, a, s, 2, 0), span(one, a, s, 0, size), self.ahead)
            send(s, a, k + 1, self.piece(ref, a, s, 2, 1), span(one, a, s, size, size), self.behind)
            send(s, a, k + 2, self.piece(ref, a, s, 1, 1), span(two, a, s, size, size), self.ahead)
            send(s, a, k + 3, self.piece(ref, a, s, 3, 0), span(two, a, s, 2 * size, size), self.behind)

        def total_mid(self, ref, one, two, s, a, k):
            size = self.share
            arrived(s, a, k)
            there = self.piece(ref, a, s, 1, 0)
            add_into(there, [there, span(one, a, s, 0, size)], size)
            send(s, a, k + 4, there, span(two, a, s, 0, size), self.ahead)
            arrived(s, a, k + 1)
            there = self.piece(ref, a, s, 3, 1)
            add_into(there, [there, span(one, a, s, size, size)], size)
            send(s, a, k + 5, there, span(two, a, s, 3 * size, size), self.behind)

        def addends(self, ref, two, s, a, pair):
            size = self.share
            return [
                self.piece(ref, a, s, 0, pair), span(two, a, s, pair * size, size),
                span(two, a, s, (2 + pair) * size, size),
            ]

        def total_pair(self, ref, two, outgoing, incoming, s, a, k):
            arrived(s, a, k + 2, k + 3, k + 4, k + 5)
            add_into(outgoing.at[a, s], self.addends(ref, two, s, a, 1 - self.pair), self.share)
            send(s, a, k + 6, outgoing.at[a, s], incoming.at[a, s], self.partner)

        def total_end(self, ref, two, incoming, s, a, k):
            arrived(s, a, k + 6)
            return self.addends(ref, two, s, a, self.pair) + [incoming.at[a, s]]

    def add_into(target, refs, count):
        @pl.loop(0, count // 16)
        def _(i):
            part = pl.ds(pl.multiple_of(i * 16, 16), 16)
            value = refs[0][part].astype(jnp.float32)
            for ref in refs[1:]:
                value = value + ref[part].astype(jnp.float32)
            target[part] = value.astype(target.dtype)

    row_ring = Ring(z, y_lo, ROW_SHARE, 0, z_next, z_back, y_near)
    col_ring = Ring(x, y_hi, COL_SHARE, core * (ROWS // 2), x_next, x_back, y_far)
    outputs = (layer_output, token_grad)

    def product(source, tile, dims, target):
        for j in range(SIDE // WIDE):
            part = pl.ds(j * WIDE, WIDE)
            other = tiles[tile, :, part] if dims is PLAIN else tiles[tile, part, :]
            target[:, part] = lax.dot_general(
                source[...], other, dims, preferred_element_type=jnp.float32
            ).astype(jnp.bfloat16)

    def find_places():
        count = lax.broadcasted_iota(jnp.int32, (1, 2 * BLK), 1)
        for a in range(2):
            loads[1 + a].wait()

            def mark(i, found):
                return jnp.where(count == (at[a, 0, i] + 1) * TILE + at[a, 1, i] + 1, i, found)

            marks[a:a + 1] = lax.fori_loop(0, CAP, mark, jnp.full((1, 2 * BLK), CAP, jnp.int32), unroll=6)
        load = pltpu.make_async_copy(marks, places, here_sem.at[6])
        load.start()
        load.wait()

    def assemble(s, a):
        if 1 in loads:
            find_places()
            del loads[1]
        loads[4 + a].wait()

        @pl.loop(0, TILE)
        def _(i):
            for j in range(TILE):
                tiles[a, pl.ds(pl.multiple_of(i * BLK, BLK), BLK), j * BLK:(j + 1) * BLK] = spare[a][
                    places[a, (i + 1) * TILE + j + 1]
                ]

    def gather(s, a):
        if 3 * a in loads:
            loads.pop(3 * a).wait()
        col_ring.spread(gathered, s, a, COL_GATHER)

    def gather_mid(s, a):
        col_ring.spread_mid(gathered, s, a, COL_GATHER)

    def gather_pass(s, a):
        col_ring.spread_pass(gathered, s, a, COL_GATHER)

    def gather_core(s, a):
        col_ring.spread_end(s, a, COL_GATHER)
        half = span(gathered, a, s, core * (ROWS // 2), ROWS // 2)
        send(s, a, CORE_GATHER, half, half, other_core)

    def rise(s, a):
        arrived(s, a, CORE_GATHER)
        product(gathered.at[a, s], a, (PLAIN, FLIPPED)[a], terms.at[a, s])
        if (s, a) in NEAR:
            row_ring.near(terms, row_two, s, a, ROW_SUM)
        else:
            row_ring.total(terms, row_one, row_two, s, a, ROW_SUM)

    def sum_mid(s, a):
        row_ring.total_mid(terms, row_one, row_two, s, a, ROW_SUM)

    def sum_pair(s, a):
        row_ring.total_pair(terms, row_two, row_send, row_pair, s, a, ROW_SUM)

    def sumb_two(s, a):
        row_ring.near_two(terms, row_two, row_pair, s, a, ROW_SUM)

    def sumb_one(s, a):
        row_ring.near_one(terms, row_two, row_one, s, a, ROW_SUM)

    def sumb_mid(s, a):
        row_ring.near_mid(terms, row_pair, row_one, s, a, ROW_SUM)

    def sumb_end(s, a):
        bend_fields(s, a, row_ring.near_end(terms, row_two, row_one, s, a, ROW_SUM))

    def sum_end(s, a):
        bend_fields(s, a, row_ring.total_end(terms, row_two, row_pair, s, a, ROW_SUM))

    def bend_fields(s, a, refs):
        own = row_ring.piece(fields, a, s, 0, y_lo)

        @pl.loop(0, ROW_SHARE // 16)
        def _(i):
            part = pl.ds(pl.multiple_of(i * 16, 16), 16)
            value = refs[0][part].astype(jnp.float32)
            for ref in refs[1:]:
                value = value + ref[part].astype(jnp.float32)
            if a == 0:
                hidden[s, part] = value
                bend = jnp.tanh(CURVE * (value + CUBIC * (value * value * value)))
                own[part] = (0.5 * value * (1.0 + bend)).astype(jnp.bfloat16)
            else:
                at = hidden[s, part]
                square = at * at
                bend = jnp.tanh(CURVE * (at + CUBIC * (square * at)))
                slope = 0.5 * (1.0 + bend) + 0.5 * at * (1.0 - bend * bend) * CURVE * (1.0 + 3.0 * CUBIC * square)
                own[part] = (slope * value).astype(jnp.bfloat16)

        if (s, a) in WIDE_FIRST:
            row_ring.wide(fields, s, a, ROW_GATHER)
        else:
            row_ring.spread(fields, s, a, ROW_GATHER)

    def sprb_mid(s, a):
        row_ring.wide_mid(fields, s, a, ROW_GATHER)

    def sprb_pass(s, a):
        row_ring.wide_pass(fields, s, a, ROW_GATHER)

    def sprb_end(s, a):
        row_ring.wide_end(s, a, ROW_GATHER)

    def spread_mid(s, a):
        row_ring.spread_mid(fields, s, a, ROW_GATHER)

    def spread_pass(s, a):
        row_ring.spread_pass(fields, s, a, ROW_GATHER)

    def spread_end(s, a):
        row_ring.spread_end(s, a, ROW_GATHER)

    def fall(s, a):
        for k in range(ROW_SUM, ROW_GATHER):
            if (s, a, k) in copies:
                copies.pop((s, a, k)).wait_send()
        for c in range(TILE):
            blocked[a, s, c + 1] = fields[a, s, :, c * BLK:(c + 1) * BLK]
        product(fields.at[a, s], 1 - a, (PLAIN, FLIPPED)[a], terms.at[a, s])
        half = span(terms, a, s, (1 - core) * (ROWS // 2), ROWS // 2)
        send(s, a, CORE_SUM, half, core_in.at[a, s], other_core)

    def core_end(s, a):
        arrived(s, a, CORE_SUM)
        half = span(terms, a, s, core * (ROWS // 2), ROWS // 2)
        add_into(half, [half, core_in.at[a, s]], ROWS // 2)
        col_ring.total(terms, col_one, col_two, s, a, COL_SUM)

    def out_mid(s, a):
        col_ring.total_mid(terms, col_one, col_two, s, a, COL_SUM)

    def out_pair(s, a):
        col_ring.total_pair(terms, col_two, col_send, col_pair, s, a, COL_SUM)

    def out_end(s, a):
        refs = col_ring.total_end(terms, col_two, col_pair, s, a, COL_SUM)
        add_into(outputs[a].at[s], refs, COL_SHARE)

    def flip(s, a):
        source = gathered.at[a, s]

        for i in range(TILE):
            flipped[a, i + 1, :, s * ROWS:(s + 1) * ROWS] = source[:, i * BLK:(i + 1) * BLK].T

    def slot(j, a):
        for i in range(j * SLOTS, (j + 1) * SLOTS):
            r, c = at[1 - a, 0, i] + 1, at[1 - a, 1, i] + 1
            left, right = (c, r) if a == 0 else (r, c)
            value = lax.dot_general(
                flipped[1 - a, left], blocked[a, :, right].reshape(TOKENS, BLK), PLAIN,
                preferred_element_type=jnp.float32,
            )
            value = (value * (1.0 / 32.0)).astype(jnp.bfloat16)
            (narrow_grad, widen_grad)[a][0, i] = value.T if a == 0 else value

    steps = {
        step.__name__: step
        for step in (
            assemble, gather, gather_mid, gather_pass, gather_core, rise, sum_mid, sum_pair, sum_end, spread_mid,
            spread_pass, spread_end, fall, core_end, out_mid, out_pair, out_end, flip, slot,
            sumb_two, sumb_one, sumb_mid, sumb_end, sprb_mid, sprb_pass, sprb_end,
        )
    }
    for index, s, a in ORDER:
        steps[STEPS[index]](s, a)
    for copy in copies.values():
        copy.wait_send()


def hand_on(*refs):
    sources, targets, sem = refs[:4], refs[4:8], refs[8]
    stores = []
    for i in range(4):
        for j in range(1 if i < 2 else CAP // SLOTS):
            part = pl.ds(j * SLOTS, SLOTS)
            source = sources[i] if i < 2 else sources[i].at[0, part]
            target = targets[i] if i < 2 else targets[i].at[0, part]
            stores.append(pltpu.make_async_copy(source, target, sem.at[i, j]))
            stores[-1].start()
    for store in stores:
        store.wait()


def local(tokens, widen_blocks, widen_pattern, narrow_blocks, narrow_pattern, cotangent):
    grouped = (STAGES, COL_SHARE, SIDE)
    anywhere, vmem = pl.BlockSpec(memory_space=pl.ANY), pl.BlockSpec(memory_space=pltpu.VMEM)
    results = (
        jax.ShapeDtypeStruct(grouped, jnp.bfloat16),
        jax.ShapeDtypeStruct(grouped, jnp.bfloat16),
        jax.ShapeDtypeStruct(widen_blocks.shape, jnp.bfloat16),
        jax.ShapeDtypeStruct(narrow_blocks.shape, jnp.bfloat16),
    )

    def room(*shape, dtype=jnp.bfloat16):
        return pltpu.VMEM((*shape, SIDE), dtype)

    outs = pl.pallas_call(
        body,
        out_shape=tuple(pltpu.VMEM(r.shape, r.dtype) for r in results),
        in_specs=[anywhere] * 6,
        out_specs=[vmem] * 4,
        scratch_shapes=[
            room(2, STAGES, ROWS),
            room(2, STAGES, ROWS),
            room(2, STAGES, ROWS),
            room(2, SIDE),
            room(2, STAGES, 2 * ROW_SHARE),
            room(2, STAGES, 4 * ROW_SHARE),
            room(2, STAGES, ROW_SHARE),
            room(2, STAGES, ROW_SHARE),
            room(2, STAGES, ROWS // 2),
            room(2, STAGES, 2 * COL_SHARE),
            room(2, STAGES, 4 * COL_SHARE),
            room(2, STAGES, COL_SHARE),
            room(2, STAGES, COL_SHARE),
            room(STAGES, ROW_SHARE, dtype=jnp.float32),
            pltpu.VMEM((CAP + 1, BLK, BLK), jnp.bfloat16),
            pltpu.VMEM((CAP + 1, BLK, BLK), jnp.bfloat16),
            pltpu.VMEM((2, TILE + 1, BLK, TOKENS), jnp.bfloat16),
            pltpu.VMEM((2, STAGES, TILE + 1, ROWS, BLK), jnp.bfloat16),
            pltpu.SMEM((2, 2, CAP), jnp.int32),
            pltpu.VMEM((2, 2 * BLK), jnp.int32),
            pltpu.SMEM((2, 2 * BLK), jnp.int32),
            pltpu.SemaphoreType.DMA((2, STAGES, COPIES)),
            pltpu.SemaphoreType.DMA((2, STAGES, COPIES)),
            pltpu.SemaphoreType.DMA((7,)),
        ],
        compiler_params=pltpu.CompilerParams(
            collective_id=0, has_side_effects=True, vmem_limit_bytes=57 * 2**20
        ),
        name="layer",
    )(
        widen_pattern[0].T, narrow_pattern[0].T, tokens.reshape(grouped), cotangent.reshape(grouped),
        widen_blocks, narrow_blocks,
    )
    outs = pl.pallas_call(
        hand_on, out_shape=results, in_specs=[vmem] * 4, out_specs=[anywhere] * 4,
        scratch_shapes=[pltpu.SemaphoreType.DMA((4, CAP // SLOTS))], name="hand_on",
    )(*(pltpu.with_memory_space_constraint(o, pltpu.VMEM) for o in outs))
    return outs[0].reshape(tokens.shape), outs[1].reshape(tokens.shape), outs[2], outs[3]


def solution(mesh):
    placed = (
        P("col", "row"),
        P("row", "col", None, None),
        P("row", "col", None),
        P("row", "col", None, None),
        P("row", "col", None),
        P("col", "row"),
    )
    return jax.shard_map(
        local,
        mesh=mesh,
        in_specs=placed,
        out_specs=(
            P("col", "row"),
            P("col", "row"),
            P("row", "col", None, None),
            P("row", "col", None, None),
        ),
        check_vma=False,
    )
```

```python
import functools

import jax
import jax.numpy as jnp
from jax import lax
from jax.experimental import pallas as pl
from jax.experimental.pallas import tpu as pltpu
from jax.sharding import PartitionSpec as P

MESH = pl.DeviceIdType.MESH
BLK = 128
TILE = 12
SIDE = BLK * TILE
CAP = 36
SLOTS = 12
TOKENS = 1024
STAGES = 4
ROWS = TOKENS // STAGES
ROW_SHARE = ROWS // 8
COL_SHARE = ROWS // 16
WIDE = 768
CURVE = 0.7978845608028654
CUBIC = 0.044715
PLAIN = (((1,), (0,)), ((), ()))
FLIPPED = (((1,), (1,)), ((), ()))
TALL = (((0,), (0,)), ((), ()))
COL_GATHER, CORE_GATHER, ROW_SUM, ROW_GATHER, CORE_SUM, COL_SUM, COPIES = 0, 7, 8, 18, 26, 27, 34


NEAR = ((0, 1), (2, 0), (2, 1), (3, 0))
WIDE_FIRST = ((1, 1), (2, 1), (3, 1))
STEPS = (
    "gather", "assemble", "gather_mid", "gather_pass", "gather_core", "rise", "sum_mid", "sum_pair", "sum_end",
    "flip", "sumb_two", "sumb_one", "spread_mid", "sumb_mid", "spread_pass", "sumb_end", "spread_end", "fall",
    "core_end", "sprb_mid", "sprb_pass", "out_mid", "sprb_end", "out_pair", "slot", "out_end",
)
ORDER = (
    (0, 0, 0), (0, 0, 1), (1, 0, 0), (0, 1, 0), (2, 0, 0), (2, 0, 1), (2, 1, 0), (3, 0, 0), (1, 0, 1), (3, 0, 1),
    (3, 1, 0), (0, 2, 1), (0, 1, 1), (0, 3, 0), (4, 0, 0), (5, 0, 0), (2, 1, 1), (4, 0, 1), (0, 2, 0), (4, 1, 0),
    (0, 3, 1), (2, 3, 0), (2, 2, 1), (5, 0, 1), (3, 1, 1), (6, 0, 0), (5, 1, 0), (3, 2, 1), (7, 0, 0), (4, 1, 1),
    (2, 2, 0), (6, 1, 0), (5, 1, 1), (2, 3, 1), (4, 2, 1), (7, 1, 0), (8, 0, 0), (6, 1, 1), (5, 2, 1), (9, 1, 1),
    (10, 0, 1), (11, 0, 1), (8, 1, 0), (12, 0, 0), (3, 2, 0), (3, 3, 0), (7, 1, 1), (9, 0, 1), (3, 3, 1), (10, 2, 1),
    (4, 2, 0), (5, 2, 0), (13, 0, 1), (14, 0, 0), (4, 3, 1), (4, 3, 0), (11, 2, 1), (15, 0, 1), (5, 3, 1), (12, 1, 0),
    (8, 1, 1), (16, 0, 0), (9, 3, 1), (5, 3, 0), (10, 2, 0), (11, 2, 0), (14, 1, 0), (17, 0, 0), (13, 2, 1),
    (13, 2, 0), (18, 0, 0), (10, 3, 0), (19, 1, 1), (6, 3, 1), (15, 2, 0), (16, 1, 0), (17, 1, 0), (9, 2, 0),
    (20, 1, 1), (18, 1, 0), (12, 0, 1), (15, 2, 1), (21, 1, 0), (14, 0, 1), (7, 3, 1), (9, 3, 0), (12, 2, 0),
    (21, 0, 0), (22, 1, 1), (11, 3, 0), (13, 3, 0), (19, 2, 1), (17, 1, 1), (16, 0, 1), (14, 2, 0), (17, 0, 1),
    (9, 0, 0), (15, 3, 0), (20, 2, 1), (8, 3, 1), (18, 0, 1), (18, 1, 1), (9, 1, 0), (16, 2, 0), (17, 2, 0),
    (12, 3, 0), (18, 2, 0), (19, 3, 1), (22, 2, 1), (17, 2, 1), (21, 1, 1), (14, 3, 0), (9, 2, 1), (20, 3, 1),
    (21, 0, 1), (23, 1, 0), (18, 2, 1), (23, 0, 0), (16, 3, 0), (21, 2, 0), (17, 3, 0), (21, 2, 1), (22, 3, 1),
    (17, 3, 1), (18, 3, 0), (24, 0, 0), (23, 0, 1), (18, 3, 1), (23, 2, 0), (23, 2, 1), (23, 1, 1), (24, 1, 0),
    (21, 3, 0), (24, 0, 1), (21, 3, 1), (25, 1, 0), (24, 2, 0), (23, 3, 0), (25, 0, 0), (25, 0, 1), (23, 3, 1),
    (25, 2, 0), (25, 2, 1), (24, 1, 1), (24, 2, 1), (25, 1, 1), (25, 3, 0), (25, 3, 1),
)


def body(
    widen_at, narrow_at, tokens, cotangent, widen_blocks, narrow_blocks,
    layer_output, token_grad, widen_grad, narrow_grad,
    gathered, terms, fields, tiles, row_one, row_two, row_pair, row_send, core_in,
    col_one, col_two, col_pair, col_send, hidden, widen_spare, narrow_spare, flipped, blocked, at, marks, places,
    send_sem, recv_sem, here_sem,
):
    row, col = lax.axis_index("row"), lax.axis_index("col")
    y_lo, z = row // 4, row % 4
    x, y_hi, core = col // 4, (col // 2) % 2, col % 2

    def on_row(pair, ring):
        return (pair * 4 + ring % 4, col)

    def on_col(ring, pair, side):
        return (row, (ring % 4) * 4 + pair * 2 + side)

    z_next, z_back, y_near = on_row(y_lo, z + 1), on_row(y_lo, z + 3), on_row(1 - y_lo, z)
    x_next, x_back = on_col(x + 1, y_hi, core), on_col(x + 3, y_hi, core)
    y_far, other_core = on_col(x, 1 - y_hi, core), on_col(x, y_hi, 1 - core)

    spare = (widen_spare, narrow_spare)
    own_rows = pl.multiple_of(core * (ROWS // 2) + (x * 2 + y_hi) * COL_SHARE, COL_SHARE)
    loads = {}
    for i, (source, target) in enumerate((
        (tokens, gathered.at[0, :, pl.ds(own_rows, COL_SHARE)]),
        (widen_at, at.at[0]),
        (narrow_at, at.at[1]),
        (cotangent, gathered.at[1, :, pl.ds(own_rows, COL_SHARE)]),
        (widen_blocks.at[0], widen_spare.at[pl.ds(0, CAP)]),
        (narrow_blocks.at[0], narrow_spare.at[pl.ds(0, CAP)]),
    )):
        loads[i] = pltpu.make_async_copy(source, target, here_sem.at[i])
        loads[i].start()

    barrier = pltpu.get_barrier_semaphore()
    partners = (z_next, z_back, y_near, x_next, x_back, y_far, other_core)
    for partner in partners:
        pl.semaphore_signal(barrier, inc=1, device_id=partner, device_id_type=MESH)

    for a in range(2):
        spare[a][CAP] = jnp.zeros((BLK, BLK), jnp.bfloat16)
        flipped[a, 0] = jnp.zeros((BLK, TOKENS), jnp.bfloat16)
        blocked[a, :, 0] = jnp.zeros((STAGES, ROWS, BLK), jnp.bfloat16)
    pl.semaphore_wait(barrier, len(partners))

    copies = {}

    def send(s, a, k, source, target, device):
        copy = pltpu.make_async_remote_copy(
            src_ref=source, dst_ref=target, send_sem=send_sem.at[a, s, k], recv_sem=recv_sem.at[a, s, k],
            device_id=device, device_id_type=MESH,
        )
        copy.start()
        copies[s, a, k] = copy

    def arrived(s, a, *ks):
        for k in ks:
            copies[s, a, k].wait_recv()

    def span(ref, a, s, start, length):
        return ref.at[a, s, pl.ds(pl.multiple_of(start, length), length)]

    class Ring:
        def __init__(self, place, pair, share, base, ahead, behind, partner):
            self.place, self.pair, self.share, self.base = place, pair, share, base
            self.ahead, self.behind, self.partner = ahead, behind, partner

        def piece(self, ref, a, s, step, pair):
            return span(ref, a, s, self.base + (((self.place + step) % 4) * 2 + pair) * self.share, self.share)

        def spread(self, ref, s, a, k):
            own = self.piece(ref, a, s, 0, self.pair)
            send(s, a, k, own, own, self.partner)
            send(s, a, k + 1, own, own, self.ahead)
            send(s, a, k + 2, own, own, self.behind)

        def spread_mid(self, ref, s, a, k):
            arrived(s, a, k)
            near = self.piece(ref, a, s, 0, 1 - self.pair)
            send(s, a, k + 3, near, near, self.ahead)
            send(s, a, k + 4, near, near, self.behind)

        def spread_pass(self, ref, s, a, k):
            arrived(s, a, k + 1)
            left = self.piece(ref, a, s, 3, self.pair)
            send(s, a, k + 5, left, left, self.ahead)
            arrived(s, a, k + 4)
            right = self.piece(ref, a, s, 1, 1 - self.pair)
            send(s, a, k + 6, right, right, self.behind)

        def spread_end(self, s, a, k):
            arrived(s, a, k + 2, k + 3, k + 5, k + 6)

        def half(self, ref, which):
            size = self.share // 2
            return ref.at[pl.ds(which * size, size)]

        def wide(self, ref, s, a, k):
            own = self.piece(ref, a, s, 0, self.pair)
            send(s, a, k, own, own, self.ahead)
            send(s, a, k + 1, own, own, self.behind)
            send(s, a, k + 4, own, own, self.partner)

        def wide_mid(self, ref, s, a, k):
            left, right = self.piece(ref, a, s, 3, self.pair), self.piece(ref, a, s, 1, self.pair)
            arrived(s, a, k)
            send(s, a, k + 2, self.half(left, 0), self.half(left, 0), self.ahead)
            arrived(s, a, k + 1)
            send(s, a, k + 3, self.half(right, 1), self.half(right, 1), self.behind)
            send(s, a, k + 5, left, left, self.partner)
            send(s, a, k + 6, right, right, self.partner)

        def wide_pass(self, ref, s, a, k):
            arrived(s, a, k + 2, k + 3)
            far = self.piece(ref, a, s, 2, self.pair)
            send(s, a, k + 7, far, far, self.partner)

        def wide_end(self, s, a, k):
            arrived(s, a, k + 4, k + 5, k + 6, k + 7)

        def near(self, ref, near, s, a, k):
            for i, step in enumerate((2, 1, 3, 0)):
                source = self.piece(ref, a, s, step, 1 - self.pair)
                send(s, a, k + i, source, span(near, a, s, step * self.share, self.share), self.partner)

        def join(self, ref, near, s, a, step):
            there = self.piece(ref, a, s, step, self.pair)
            add_into(there, [there, span(near, a, s, step * self.share, self.share)], self.share)
            return there

        def near_two(self, ref, near, one, s, a, k):
            arrived(s, a, k)
            there = self.join(ref, near, s, a, 2)
            send(s, a, k + 4, self.half(there, 0), self.half(one.at[a, s], 0), self.ahead)
            send(s, a, k + 5, self.half(there, 1), self.half(one.at[a, s], 1), self.behind)

        def near_one(self, ref, near, two, s, a, k):
            size = self.share
            arrived(s, a, k + 1)
            there = self.join(ref, near, s, a, 1)
            send(s, a, k + 6, self.half(there, 1), self.half(span(two, a, s, 0, size), 1), self.ahead)
            arrived(s, a, k + 2)
            there = self.join(ref, near, s, a, 3)
            send(s, a, k + 7, self.half(there, 0), self.half(span(two, a, s, size, size), 0), self.behind)

        def near_mid(self, ref, one, two, s, a, k):
            size = self.share
            arrived(s, a, k + 4)
            there = self.half(self.piece(ref, a, s, 1, self.pair), 0)
            add_into(there, [there, self.half(one.at[a, s], 0)], size // 2)
            send(s, a, k + 8, there, self.half(span(two, a, s, 0, size), 0), self.ahead)
            arrived(s, a, k + 5)
            there = self.half(self.piece(ref, a, s, 3, self.pair), 1)
            add_into(there, [there, self.half(one.at[a, s], 1)], size // 2)
            send(s, a, k + 9, there, self.half(span(two, a, s, size, size), 1), self.behind)

        def near_end(self, ref, near, two, s, a, k):
            size = self.share
            arrived(s, a, k + 3, k + 6, k + 7, k + 8, k + 9)
            return [
                self.piece(ref, a, s, 0, self.pair), span(near, a, s, 0, size),
                span(two, a, s, 0, size), span(two, a, s, size, size),
            ]

        def total(self, ref, one, two, s, a, k):
            size = self.share
            send(s, a, k, self.piece(ref, a, s, 2, 0), span(one, a, s, 0, size), self.ahead)
            send(s, a, k + 1, self.piece(ref, a, s, 2, 1), span(one, a, s, size, size), self.behind)
            send(s, a, k + 2, self.piece(ref, a, s, 1, 1), span(two, a, s, size, size), self.ahead)
            send(s, a, k + 3, self.piece(ref, a, s, 3, 0), span(two, a, s, 2 * size, size), self.behind)

        def total_mid(self, ref, one, two, s, a, k):
            size = self.share
            arrived(s, a, k)
            there = self.piece(ref, a, s, 1, 0)
            add_into(there, [there, span(one, a, s, 0, size)], size)
            send(s, a, k + 4, there, span(two, a, s, 0, size), self.ahead)
            arrived(s, a, k + 1)
            there = self.piece(ref, a, s, 3, 1)
            add_into(there, [there, span(one, a, s, size, size)], size)
            send(s, a, k + 5, there, span(two, a, s, 3 * size, size), self.behind)

        def addends(self, ref, two, s, a, pair):
            size = self.share
            return [
                self.piece(ref, a, s, 0, pair), span(two, a, s, pair * size, size),
                span(two, a, s, (2 + pair) * size, size),
            ]

        def total_pair(self, ref, two, outgoing, incoming, s, a, k):
            arrived(s, a, k + 2, k + 3, k + 4, k + 5)
            add_into(outgoing.at[a, s], self.addends(ref, two, s, a, 1 - self.pair), self.share)
            send(s, a, k + 6, outgoing.at[a, s], incoming.at[a, s], self.partner)

        def total_end(self, ref, two, incoming, s, a, k):
            arrived(s, a, k + 6)
            return self.addends(ref, two, s, a, self.pair) + [incoming.at[a, s]]

    def add_into(target, refs, count):
        @pl.loop(0, count // 16)
        def _(i):
            part = pl.ds(pl.multiple_of(i * 16, 16), 16)
            value = refs[0][part].astype(jnp.float32)
            for ref in refs[1:]:
                value = value + ref[part].astype(jnp.float32)
            target[part] = value.astype(target.dtype)

    row_ring = Ring(z, y_lo, ROW_SHARE, 0, z_next, z_back, y_near)
    col_ring = Ring(x, y_hi, COL_SHARE, core * (ROWS // 2), x_next, x_back, y_far)
    outputs = (layer_output, token_grad)

    def product(source, tile, dims, target):
        for j in range(SIDE // WIDE):
            part = pl.ds(j * WIDE, WIDE)
            other = tiles[tile, :, part] if dims is PLAIN else tiles[tile, part, :]
            target[:, part] = lax.dot_general(
                source[...], other, dims, preferred_element_type=jnp.float32
            ).astype(jnp.bfloat16)

    def find_places():
        count = lax.broadcasted_iota(jnp.int32, (1, 2 * BLK), 1)
        for a in range(2):
            loads[1 + a].wait()

            def mark(i, found):
                return jnp.where(count == (at[a, 0, i] + 1) * TILE + at[a, 1, i] + 1, i, found)

            marks[a:a + 1] = lax.fori_loop(0, CAP, mark, jnp.full((1, 2 * BLK), CAP, jnp.int32), unroll=6)
        load = pltpu.make_async_copy(marks, places, here_sem.at[6])
        load.start()
        load.wait()

    def assemble(s, a):
        if 1 in loads:
            find_places()
            del loads[1]
        loads[4 + a].wait()

        @pl.loop(0, TILE)
        def _(i):
            for j in range(TILE):
                tiles[a, pl.ds(pl.multiple_of(i * BLK, BLK), BLK), j * BLK:(j + 1) * BLK] = spare[a][
                    places[a, (i + 1) * TILE + j + 1]
                ]

    def gather(s, a):
        if 3 * a in loads:
            loads.pop(3 * a).wait()
        col_ring.spread(gathered, s, a, COL_GATHER)

    def gather_mid(s, a):
        col_ring.spread_mid(gathered, s, a, COL_GATHER)

    def gather_pass(s, a):
        col_ring.spread_pass(gathered, s, a, COL_GATHER)

    def gather_core(s, a):
        col_ring.spread_end(s, a, COL_GATHER)
        half = span(gathered, a, s, core * (ROWS // 2), ROWS // 2)
        send(s, a, CORE_GATHER, half, half, other_core)

    def rise(s, a):
        arrived(s, a, CORE_GATHER)
        product(gathered.at[a, s], a, (PLAIN, FLIPPED)[a], terms.at[a, s])
        if (s, a) in NEAR:
            row_ring.near(terms, row_two, s, a, ROW_SUM)
        else:
            row_ring.total(terms, row_one, row_two, s, a, ROW_SUM)

    def sum_mid(s, a):
        row_ring.total_mid(terms, row_one, row_two, s, a, ROW_SUM)

    def sum_pair(s, a):
        row_ring.total_pair(terms, row_two, row_send, row_pair, s, a, ROW_SUM)

    def sumb_two(s, a):
        row_ring.near_two(terms, row_two, row_pair, s, a, ROW_SUM)

    def sumb_one(s, a):
        row_ring.near_one(terms, row_two, row_one, s, a, ROW_SUM)

    def sumb_mid(s, a):
        row_ring.near_mid(terms, row_pair, row_one, s, a, ROW_SUM)

    def sumb_end(s, a):
        bend_fields(s, a, row_ring.near_end(terms, row_two, row_one, s, a, ROW_SUM))

    def sum_end(s, a):
        bend_fields(s, a, row_ring.total_end(terms, row_two, row_pair, s, a, ROW_SUM))

    def bend_fields(s, a, refs):
        own = row_ring.piece(fields, a, s, 0, y_lo)

        @pl.loop(0, ROW_SHARE // 16)
        def _(i):
            part = pl.ds(pl.multiple_of(i * 16, 16), 16)
            value = refs[0][part].astype(jnp.float32)
            for ref in refs[1:]:
                value = value + ref[part].astype(jnp.float32)
            if a == 0:
                hidden[s, part] = value
                bend = jnp.tanh(CURVE * (value + CUBIC * (value * value * value)))
                own[part] = (0.5 * value * (1.0 + bend)).astype(jnp.bfloat16)
            else:
                at = hidden[s, part]
                square = at * at
                bend = jnp.tanh(CURVE * (at + CUBIC * (square * at)))
                slope = 0.5 * (1.0 + bend) + 0.5 * at * (1.0 - bend * bend) * CURVE * (1.0 + 3.0 * CUBIC * square)
                own[part] = (slope * value).astype(jnp.bfloat16)

        if (s, a) in WIDE_FIRST:
            row_ring.wide(fields, s, a, ROW_GATHER)
        else:
            row_ring.spread(fields, s, a, ROW_GATHER)

    def sprb_mid(s, a):
        row_ring.wide_mid(fields, s, a, ROW_GATHER)

    def sprb_pass(s, a):
        row_ring.wide_pass(fields, s, a, ROW_GATHER)

    def sprb_end(s, a):
        row_ring.wide_end(s, a, ROW_GATHER)

    def spread_mid(s, a):
        row_ring.spread_mid(fields, s, a, ROW_GATHER)

    def spread_pass(s, a):
        row_ring.spread_pass(fields, s, a, ROW_GATHER)

    def spread_end(s, a):
        row_ring.spread_end(s, a, ROW_GATHER)

    def fall(s, a):
        for k in range(ROW_SUM, ROW_GATHER):
            if (s, a, k) in copies:
                copies.pop((s, a, k)).wait_send()
        for c in range(TILE):
            blocked[a, s, c + 1] = fields[a, s, :, c * BLK:(c + 1) * BLK]
        product(fields.at[a, s], 1 - a, (PLAIN, FLIPPED)[a], terms.at[a, s])
        half = span(terms, a, s, (1 - core) * (ROWS // 2), ROWS // 2)
        send(s, a, CORE_SUM, half, core_in.at[a, s], other_core)

    def core_end(s, a):
        arrived(s, a, CORE_SUM)
        half = span(terms, a, s, core * (ROWS // 2), ROWS // 2)
        add_into(half, [half, core_in.at[a, s]], ROWS // 2)
        col_ring.total(terms, col_one, col_two, s, a, COL_SUM)

    def out_mid(s, a):
        col_ring.total_mid(terms, col_one, col_two, s, a, COL_SUM)

    def out_pair(s, a):
        col_ring.total_pair(terms, col_two, col_send, col_pair, s, a, COL_SUM)

    def out_end(s, a):
        refs = col_ring.total_end(terms, col_two, col_pair, s, a, COL_SUM)
        add_into(outputs[a].at[s], refs, COL_SHARE)

    def flip(s, a):
        source = gathered.at[a, s]

        for i in range(TILE):
            flipped[a, i + 1, :, s * ROWS:(s + 1) * ROWS] = source[:, i * BLK:(i + 1) * BLK].T

    def slot(j, a):
        for i in range(j * SLOTS, (j + 1) * SLOTS):
            r, c = at[1 - a, 0, i] + 1, at[1 - a, 1, i] + 1
            left, right = (c, r) if a == 0 else (r, c)
            value = lax.dot_general(
                flipped[1 - a, left], blocked[a, :, right].reshape(TOKENS, BLK), PLAIN,
                preferred_element_type=jnp.float32,
            )
            value = (value * (1.0 / 32.0)).astype(jnp.bfloat16)
            (narrow_grad, widen_grad)[a][0, i] = value.T if a == 0 else value

    steps = {
        step.__name__: step
        for step in (
            assemble, gather, gather_mid, gather_pass, gather_core, rise, sum_mid, sum_pair, sum_end, spread_mid,
            spread_pass, spread_end, fall, core_end, out_mid, out_pair, out_end, flip, slot,
            sumb_two, sumb_one, sumb_mid, sumb_end, sprb_mid, sprb_pass, sprb_end,
        )
    }
    for index, s, a in ORDER:
        steps[STEPS[index]](s, a)
    for copy in copies.values():
        copy.wait_send()


def hand_on(*refs):
    sources, targets, sem = refs[:4], refs[4:8], refs[8]
    stores = []
    for i in range(4):
        for j in range(1 if i < 2 else CAP // SLOTS):
            part = pl.ds(j * SLOTS, SLOTS)
            source = sources[i] if i < 2 else sources[i].at[0, part]
            target = targets[i] if i < 2 else targets[i].at[0, part]
            stores.append(pltpu.make_async_copy(source, target, sem.at[i, j]))
            stores[-1].start()
    for store in stores:
        store.wait()


def local(tokens, widen_blocks, widen_pattern, narrow_blocks, narrow_pattern, cotangent):
    grouped = (STAGES, COL_SHARE, SIDE)
    anywhere, vmem = pl.BlockSpec(memory_space=pl.ANY), pl.BlockSpec(memory_space=pltpu.VMEM)
    results = (
        jax.ShapeDtypeStruct(grouped, jnp.bfloat16),
        jax.ShapeDtypeStruct(grouped, jnp.bfloat16),
        jax.ShapeDtypeStruct(widen_blocks.shape, jnp.bfloat16),
        jax.ShapeDtypeStruct(narrow_blocks.shape, jnp.bfloat16),
    )

    def room(*shape, dtype=jnp.bfloat16):
        return pltpu.VMEM((*shape, SIDE), dtype)

    outs = pl.pallas_call(
        body,
        out_shape=tuple(pltpu.VMEM(r.shape, r.dtype) for r in results),
        in_specs=[anywhere] * 6,
        out_specs=[vmem] * 4,
        scratch_shapes=[
            room(2, STAGES, ROWS),
            room(2, STAGES, ROWS),
            room(2, STAGES, ROWS),
            room(2, SIDE),
            room(2, STAGES, 2 * ROW_SHARE),
            room(2, STAGES, 4 * ROW_SHARE),
            room(2, STAGES, ROW_SHARE),
            room(2, STAGES, ROW_SHARE),
            room(2, STAGES, ROWS // 2),
            room(2, STAGES, 2 * COL_SHARE),
            room(2, STAGES, 4 * COL_SHARE),
            room(2, STAGES, COL_SHARE),
            room(2, STAGES, COL_SHARE),
            room(STAGES, ROW_SHARE, dtype=jnp.float32),
            pltpu.VMEM((CAP + 1, BLK, BLK), jnp.bfloat16),
            pltpu.VMEM((CAP + 1, BLK, BLK), jnp.bfloat16),
            pltpu.VMEM((2, TILE + 1, BLK, TOKENS), jnp.bfloat16),
            pltpu.VMEM((2, STAGES, TILE + 1, ROWS, BLK), jnp.bfloat16),
            pltpu.SMEM((2, 2, CAP), jnp.int32),
            pltpu.VMEM((2, 2 * BLK), jnp.int32),
            pltpu.SMEM((2, 2 * BLK), jnp.int32),
            pltpu.SemaphoreType.DMA((2, STAGES, COPIES)),
            pltpu.SemaphoreType.DMA((2, STAGES, COPIES)),
            pltpu.SemaphoreType.DMA((7,)),
        ],
        compiler_params=pltpu.CompilerParams(
            collective_id=0, has_side_effects=True, vmem_limit_bytes=57 * 2**20
        ),
        name="layer",
    )(
        widen_pattern[0].T, narrow_pattern[0].T, tokens.reshape(grouped), cotangent.reshape(grouped),
        widen_blocks, narrow_blocks,
    )
    outs = pl.pallas_call(
        hand_on, out_shape=results, in_specs=[vmem] * 4, out_specs=[anywhere] * 4,
        scratch_shapes=[pltpu.SemaphoreType.DMA((4, CAP // SLOTS))], name="hand_on",
    )(*(pltpu.with_memory_space_constraint(o, pltpu.VMEM) for o in outs))
    return outs[0].reshape(tokens.shape), outs[1].reshape(tokens.shape), outs[2], outs[3]


def solution(mesh):
    placed = (
        P("col", "row"),
        P("row", "col", None, None),
        P("row", "col", None),
        P("row", "col", None, None),
        P("row", "col", None),
        P("col", "row"),
    )
    return jax.shard_map(
        local,
        mesh=mesh,
        in_specs=placed,
        out_specs=(
            P("col", "row"),
            P("col", "row"),
            P("row", "col", None, None),
            P("row", "col", None, None),
        ),
        check_vma=False,
    )
```

```python
import functools

import jax
import jax.numpy as jnp
from jax import lax
from jax.experimental import pallas as pl
from jax.experimental.pallas import tpu as pltpu
from jax.sharding import PartitionSpec as P

MESH = pl.DeviceIdType.MESH
BLK = 128
TILE = 12
SIDE = BLK * TILE
CAP = 36
SLOTS = 12
TOKENS = 1024
STAGES = 4
ROWS = TOKENS // STAGES
ROW_SHARE = ROWS // 8
COL_SHARE = ROWS // 16
WIDE = 768
CURVE = 0.7978845608028654
CUBIC = 0.044715
PLAIN = (((1,), (0,)), ((), ()))
FLIPPED = (((1,), (1,)), ((), ()))
TALL = (((0,), (0,)), ((), ()))
COL_GATHER, CORE_GATHER, ROW_SUM, ROW_GATHER, CORE_SUM, COL_SUM, COPIES = 0, 7, 8, 18, 26, 27, 34


NEAR = ((0, 1), (2, 0), (2, 1), (3, 0))
WIDE_FIRST = ((1, 1), (2, 1), (3, 1))
STEPS = (
    "gather", "assemble", "gather_mid", "gather_pass", "gather_core", "rise", "sum_mid", "sum_pair", "sum_end",
    "flip", "sumb_two", "sumb_one", "spread_mid", "sumb_mid", "spread_pass", "sumb_end", "spread_end", "fall",
    "core_end", "sprb_mid", "sprb_pass", "out_mid", "sprb_end", "out_pair", "slot", "out_end",
)
ORDER = (
    (0, 0, 0), (0, 0, 1), (1, 0, 0), (0, 1, 0), (2, 0, 0), (2, 0, 1), (2, 1, 0), (3, 0, 0), (1, 0, 1), (3, 0, 1),
    (3, 1, 0), (0, 2, 1), (0, 1, 1), (0, 3, 0), (4, 0, 0), (5, 0, 0), (2, 1, 1), (4, 0, 1), (0, 2, 0), (4, 1, 0),
    (0, 3, 1), (2, 3, 0), (2, 2, 1), (5, 0, 1), (3, 1, 1), (6, 0, 0), (5, 1, 0), (3, 2, 1), (7, 0, 0), (4, 1, 1),
    (2, 2, 0), (6, 1, 0), (5, 1, 1), (2, 3, 1), (4, 2, 1), (7, 1, 0), (8, 0, 0), (6, 1, 1), (5, 2, 1), (9, 1, 1),
    (10, 0, 1), (11, 0, 1), (8, 1, 0), (12, 0, 0), (3, 2, 0), (3, 3, 0), (7, 1, 1), (9, 0, 1), (3, 3, 1), (10, 2, 1),
    (4, 2, 0), (5, 2, 0), (13, 0, 1), (14, 0, 0), (4, 3, 1), (4, 3, 0), (11, 2, 1), (15, 0, 1), (5, 3, 1), (12, 1, 0),
    (8, 1, 1), (16, 0, 0), (9, 3, 1), (5, 3, 0), (10, 2, 0), (11, 2, 0), (14, 1, 0), (17, 0, 0), (13, 2, 1),
    (13, 2, 0), (18, 0, 0), (10, 3, 0), (19, 1, 1), (6, 3, 1), (15, 2, 0), (16, 1, 0), (17, 1, 0), (9, 2, 0),
    (20, 1, 1), (18, 1, 0), (12, 0, 1), (15, 2, 1), (21, 1, 0), (14, 0, 1), (7, 3, 1), (9, 3, 0), (12, 2, 0),
    (21, 0, 0), (22, 1, 1), (11, 3, 0), (13, 3, 0), (19, 2, 1), (17, 1, 1), (16, 0, 1), (14, 2, 0), (17, 0, 1),
    (9, 0, 0), (15, 3, 0), (20, 2, 1), (8, 3, 1), (18, 0, 1), (18, 1, 1), (9, 1, 0), (16, 2, 0), (17, 2, 0),
    (12, 3, 0), (18, 2, 0), (19, 3, 1), (22, 2, 1), (17, 2, 1), (21, 1, 1), (14, 3, 0), (9, 2, 1), (20, 3, 1),
    (21, 0, 1), (23, 1, 0), (18, 2, 1), (23, 0, 0), (16, 3, 0), (21, 2, 0), (17, 3, 0), (21, 2, 1), (22, 3, 1),
    (17, 3, 1), (18, 3, 0), (24, 0, 0), (23, 0, 1), (18, 3, 1), (23, 2, 0), (23, 2, 1), (23, 1, 1), (24, 1, 0),
    (21, 3, 0), (24, 0, 1), (21, 3, 1), (25, 1, 0), (24, 2, 0), (23, 3, 0), (25, 0, 0), (25, 0, 1), (23, 3, 1),
    (25, 2, 0), (25, 2, 1), (24, 1, 1), (24, 2, 1), (25, 1, 1), (25, 3, 0), (25, 3, 1),
)


def body(
    widen_at, narrow_at, tokens, cotangent, widen_blocks, narrow_blocks,
    layer_output, token_grad, widen_grad, narrow_grad,
    gathered, terms, fields, tiles, row_one, row_two, row_pair, row_send, core_in,
    col_one, col_two, col_pair, col_send, hidden, widen_spare, narrow_spare, flipped, blocked, at, marks, places,
    send_sem, recv_sem, here_sem,
):
    row, col = lax.axis_index("row"), lax.axis_index("col")
    y_lo, z = row // 4, row % 4
    x, y_hi, core = col // 4, (col // 2) % 2, col % 2

    def on_row(pair, ring):
        return (pair * 4 + ring % 4, col)

    def on_col(ring, pair, side):
        return (row, (ring % 4) * 4 + pair * 2 + side)

    z_next, z_back, y_near = on_row(y_lo, z + 1), on_row(y_lo, z + 3), on_row(1 - y_lo, z)
    x_next, x_back = on_col(x + 1, y_hi, core), on_col(x + 3, y_hi, core)
    y_far, other_core = on_col(x, 1 - y_hi, core), on_col(x, y_hi, 1 - core)

    spare = (widen_spare, narrow_spare)
    own_rows = pl.multiple_of(core * (ROWS // 2) + (x * 2 + y_hi) * COL_SHARE, COL_SHARE)
    loads = {}
    for i, (source, target) in enumerate((
        (tokens, gathered.at[0, :, pl.ds(own_rows, COL_SHARE)]),
        (widen_at, at.at[0]),
        (narrow_at, at.at[1]),
        (cotangent, gathered.at[1, :, pl.ds(own_rows, COL_SHARE)]),
        (widen_blocks.at[0], widen_spare.at[pl.ds(0, CAP)]),
        (narrow_blocks.at[0], narrow_spare.at[pl.ds(0, CAP)]),
    )):
        loads[i] = pltpu.make_async_copy(source, target, here_sem.at[i])
        loads[i].start()

    barrier = pltpu.get_barrier_semaphore()
    partners = (z_next, z_back, y_near, x_next, x_back, y_far, other_core)
    for partner in partners:
        pl.semaphore_signal(barrier, inc=1, device_id=partner, device_id_type=MESH)

    for a in range(2):
        spare[a][CAP] = jnp.zeros((BLK, BLK), jnp.bfloat16)
        flipped[a, 0] = jnp.zeros((BLK, TOKENS), jnp.bfloat16)
        blocked[a, :, 0] = jnp.zeros((STAGES, ROWS, BLK), jnp.bfloat16)
    pl.semaphore_wait(barrier, len(partners))

    copies = {}

    def send(s, a, k, source, target, device):
        copy = pltpu.make_async_remote_copy(
            src_ref=source, dst_ref=target, send_sem=send_sem.at[a, s, k], recv_sem=recv_sem.at[a, s, k],
            device_id=device, device_id_type=MESH,
        )
        copy.start()
        copies[s, a, k] = copy

    def arrived(s, a, *ks):
        for k in ks:
            copies[s, a, k].wait_recv()

    def span(ref, a, s, start, length):
        return ref.at[a, s, pl.ds(pl.multiple_of(start, length), length)]

    class Ring:
        def __init__(self, place, pair, share, base, ahead, behind, partner):
            self.place, self.pair, self.share, self.base = place, pair, share, base
            self.ahead, self.behind, self.partner = ahead, behind, partner

        def piece(self, ref, a, s, step, pair):
            return span(ref, a, s, self.base + (((self.place + step) % 4) * 2 + pair) * self.share, self.share)

        def spread(self, ref, s, a, k):
            own = self.piece(ref, a, s, 0, self.pair)
            send(s, a, k, own, own, self.partner)
            send(s, a, k + 1, own, own, self.ahead)
            send(s, a, k + 2, own, own, self.behind)

        def spread_mid(self, ref, s, a, k):
            arrived(s, a, k)
            near = self.piece(ref, a, s, 0, 1 - self.pair)
            send(s, a, k + 3, near, near, self.ahead)
            send(s, a, k + 4, near, near, self.behind)

        def spread_pass(self, ref, s, a, k):
            arrived(s, a, k + 1)
            left = self.piece(ref, a, s, 3, self.pair)
            send(s, a, k + 5, left, left, self.ahead)
            arrived(s, a, k + 4)
            right = self.piece(ref, a, s, 1, 1 - self.pair)
            send(s, a, k + 6, right, right, self.behind)

        def spread_end(self, s, a, k):
            arrived(s, a, k + 2, k + 3, k + 5, k + 6)

        def half(self, ref, which):
            size = self.share // 2
            return ref.at[pl.ds(which * size, size)]

        def wide(self, ref, s, a, k):
            own = self.piece(ref, a, s, 0, self.pair)
            send(s, a, k, own, own, self.ahead)
            send(s, a, k + 1, own, own, self.behind)
            send(s, a, k + 4, own, own, self.partner)

        def wide_mid(self, ref, s, a, k):
            left, right = self.piece(ref, a, s, 3, self.pair), self.piece(ref, a, s, 1, self.pair)
            arrived(s, a, k)
            send(s, a, k + 2, self.half(left, 0), self.half(left, 0), self.ahead)
            arrived(s, a, k + 1)
            send(s, a, k + 3, self.half(right, 1), self.half(right, 1), self.behind)
            send(s, a, k + 5, left, left, self.partner)
            send(s, a, k + 6, right, right, self.partner)

        def wide_pass(self, ref, s, a, k):
            arrived(s, a, k + 2, k + 3)
            far = self.piece(ref, a, s, 2, self.pair)
            send(s, a, k + 7, far, far, self.partner)

        def wide_end(self, s, a, k):
            arrived(s, a, k + 4, k + 5, k + 6, k + 7)

        def near(self, ref, near, s, a, k):
            for i, step in enumerate((2, 1, 3, 0)):
                source = self.piece(ref, a, s, step, 1 - self.pair)
                send(s, a, k + i, source, span(near, a, s, step * self.share, self.share), self.partner)

        def join(self, ref, near, s, a, step):
            there = self.piece(ref, a, s, step, self.pair)
            add_into(there, [there, span(near, a, s, step * self.share, self.share)], self.share)
            return there

        def near_two(self, ref, near, one, s, a, k):
            arrived(s, a, k)
            there = self.join(ref, near, s, a, 2)
            send(s, a, k + 4, self.half(there, 0), self.half(one.at[a, s], 0), self.ahead)
            send(s, a, k + 5, self.half(there, 1), self.half(one.at[a, s], 1), self.behind)

        def near_one(self, ref, near, two, s, a, k):
            size = self.share
            arrived(s, a, k + 1)
            there = self.join(ref, near, s, a, 1)
            send(s, a, k + 6, self.half(there, 1), self.half(span(two, a, s, 0, size), 1), self.ahead)
            arrived(s, a, k + 2)
            there = self.join(ref, near, s, a, 3)
            send(s, a, k + 7, self.half(there, 0), self.half(span(two, a, s, size, size), 0), self.behind)

        def near_mid(self, ref, one, two, s, a, k):
            size = self.share
            arrived(s, a, k + 4)
            there = self.half(self.piece(ref, a, s, 1, self.pair), 0)
            add_into(there, [there, self.half(one.at[a, s], 0)], size // 2)
            send(s, a, k + 8, there, self.half(span(two, a, s, 0, size), 0), self.ahead)
            arrived(s, a, k + 5)
            there = self.half(self.piece(ref, a, s, 3, self.pair), 1)
            add_into(there, [there, self.half(one.at[a, s], 1)], size // 2)
            send(s, a, k + 9, there, self.half(span(two, a, s, size, size), 1), self.behind)

        def near_end(self, ref, near, two, s, a, k):
            size = self.share
            arrived(s, a, k + 3, k + 6, k + 7, k + 8, k + 9)
            return [
                self.piece(ref, a, s, 0, self.pair), span(near, a, s, 0, size),
                span(two, a, s, 0, size), span(two, a, s, size, size),
            ]

        def total(self, ref, one, two, s, a, k):
            size = self.share
            send(s, a, k, self.piece(ref, a, s, 2, 0), span(one, a, s, 0, size), self.ahead)
            send(s, a, k + 1, self.piece(ref, a, s, 2, 1), span(one, a, s, size, size), self.behind)
            send(s, a, k + 2, self.piece(ref, a, s, 1, 1), span(two, a, s, size, size), self.ahead)
            send(s, a, k + 3, self.piece(ref, a, s, 3, 0), span(two, a, s, 2 * size, size), self.behind)

        def total_mid(self, ref, one, two, s, a, k):
            size = self.share
            arrived(s, a, k)
            there = self.piece(ref, a, s, 1, 0)
            add_into(there, [there, span(one, a, s, 0, size)], size)
            send(s, a, k + 4, there, span(two, a, s, 0, size), self.ahead)
            arrived(s, a, k + 1)
            there = self.piece(ref, a, s, 3, 1)
            add_into(there, [there, span(one, a, s, size, size)], size)
            send(s, a, k + 5, there, span(two, a, s, 3 * size, size), self.behind)

        def addends(self, ref, two, s, a, pair):
            size = self.share
            return [
                self.piece(ref, a, s, 0, pair), span(two, a, s, pair * size, size),
                span(two, a, s, (2 + pair) * size, size),
            ]

        def total_pair(self, ref, two, outgoing, incoming, s, a, k):
            arrived(s, a, k + 2, k + 3, k + 4, k + 5)
            add_into(outgoing.at[a, s], self.addends(ref, two, s, a, 1 - self.pair), self.share)
            send(s, a, k + 6, outgoing.at[a, s], incoming.at[a, s], self.partner)

        def total_end(self, ref, two, incoming, s, a, k):
            arrived(s, a, k + 6)
            return self.addends(ref, two, s, a, self.pair) + [incoming.at[a, s]]

    def add_into(target, refs, count):
        @pl.loop(0, count // 16)
        def _(i):
            part = pl.ds(pl.multiple_of(i * 16, 16), 16)
            value = refs[0][part].astype(jnp.float32)
            for ref in refs[1:]:
                value = value + ref[part].astype(jnp.float32)
            target[part] = value.astype(target.dtype)

    row_ring = Ring(z, y_lo, ROW_SHARE, 0, z_next, z_back, y_near)
    col_ring = Ring(x, y_hi, COL_SHARE, core * (ROWS // 2), x_next, x_back, y_far)
    outputs = (layer_output, token_grad)

    def product(source, tile, dims, target):
        for j in range(SIDE // WIDE):
            part = pl.ds(j * WIDE, WIDE)
            other = tiles[tile, :, part] if dims is PLAIN else tiles[tile, part, :]
            target[:, part] = lax.dot_general(
                source[...], other, dims, preferred_element_type=jnp.float32
            ).astype(jnp.bfloat16)

    def find_places():
        count = lax.broadcasted_iota(jnp.int32, (1, 2 * BLK), 1)
        for a in range(2):
            loads[1 + a].wait()

            def mark(i, found):
                return jnp.where(count == (at[a, 0, i] + 1) * TILE + at[a, 1, i] + 1, i, found)

            marks[a:a + 1] = lax.fori_loop(0, CAP, mark, jnp.full((1, 2 * BLK), CAP, jnp.int32), unroll=6)
        load = pltpu.make_async_copy(marks, places, here_sem.at[6])
        load.start()
        load.wait()

    def assemble(s, a):
        if 1 in loads:
            find_places()
            del loads[1]
        loads[4 + a].wait()

        @pl.loop(0, TILE)
        def _(i):
            for j in range(TILE):
                tiles[a, pl.ds(pl.multiple_of(i * BLK, BLK), BLK), j * BLK:(j + 1) * BLK] = spare[a][
                    places[a, (i + 1) * TILE + j + 1]
                ]

    def gather(s, a):
        if 3 * a in loads:
            loads.pop(3 * a).wait()
        col_ring.spread(gathered, s, a, COL_GATHER)

    def gather_mid(s, a):
        col_ring.spread_mid(gathered, s, a, COL_GATHER)

    def gather_pass(s, a):
        col_ring.spread_pass(gathered, s, a, COL_GATHER)

    def gather_core(s, a):
        col_ring.spread_end(s, a, COL_GATHER)
        half = span(gathered, a, s, core * (ROWS // 2), ROWS // 2)
        send(s, a, CORE_GATHER, half, half, other_core)

    def rise(s, a):
        arrived(s, a, CORE_GATHER)
        product(gathered.at[a, s], a, (PLAIN, FLIPPED)[a], terms.at[a, s])
        if (s, a) in NEAR:
            row_ring.near(terms, row_two, s, a, ROW_SUM)
        else:
            row_ring.total(terms, row_one, row_two, s, a, ROW_SUM)

    def sum_mid(s, a):
        row_ring.total_mid(terms, row_one, row_two, s, a, ROW_SUM)

    def sum_pair(s, a):
        row_ring.total_pair(terms, row_two, row_send, row_pair, s, a, ROW_SUM)

    def sumb_two(s, a):
        row_ring.near_two(terms, row_two, row_pair, s, a, ROW_SUM)

    def sumb_one(s, a):
        row_ring.near_one(terms, row_two, row_one, s, a, ROW_SUM)

    def sumb_mid(s, a):
        row_ring.near_mid(terms, row_pair, row_one, s, a, ROW_SUM)

    def sumb_end(s, a):
        bend_fields(s, a, row_ring.near_end(terms, row_two, row_one, s, a, ROW_SUM))

    def sum_end(s, a):
        bend_fields(s, a, row_ring.total_end(terms, row_two, row_pair, s, a, ROW_SUM))

    def bend_fields(s, a, refs):
        own = row_ring.piece(fields, a, s, 0, y_lo)

        @pl.loop(0, ROW_SHARE // 16)
        def _(i):
            part = pl.ds(pl.multiple_of(i * 16, 16), 16)
            value = refs[0][part].astype(jnp.float32)
            for ref in refs[1:]:
                value = value + ref[part].astype(jnp.float32)
            if a == 0:
                hidden[s, part] = value
                bend = jnp.tanh(CURVE * (value + CUBIC * (value * value * value)))
                own[part] = (0.5 * value * (1.0 + bend)).astype(jnp.bfloat16)
            else:
                at = hidden[s, part]
                square = at * at
                bend = jnp.tanh(CURVE * (at + CUBIC * (square * at)))
                slope = 0.5 * (1.0 + bend) + 0.5 * at * (1.0 - bend * bend) * CURVE * (1.0 + 3.0 * CUBIC * square)
                own[part] = (slope * value).astype(jnp.bfloat16)

        if (s, a) in WIDE_FIRST:
            row_ring.wide(fields, s, a, ROW_GATHER)
        else:
            row_ring.spread(fields, s, a, ROW_GATHER)

    def sprb_mid(s, a):
        row_ring.wide_mid(fields, s, a, ROW_GATHER)

    def sprb_pass(s, a):
        row_ring.wide_pass(fields, s, a, ROW_GATHER)

    def sprb_end(s, a):
        row_ring.wide_end(s, a, ROW_GATHER)

    def spread_mid(s, a):
        row_ring.spread_mid(fields, s, a, ROW_GATHER)

    def spread_pass(s, a):
        row_ring.spread_pass(fields, s, a, ROW_GATHER)

    def spread_end(s, a):
        row_ring.spread_end(s, a, ROW_GATHER)

    def fall(s, a):
        for k in range(ROW_SUM, ROW_GATHER):
            if (s, a, k) in copies:
                copies.pop((s, a, k)).wait_send()
        near, far = core * (ROWS // 2), (1 - core) * (ROWS // 2)
        half = span(terms, a, s, far, ROWS // 2)
        dims = (PLAIN, FLIPPED)[a]
        if s == STAGES - 1:
            product(span(fields, a, s, far, ROWS // 2), 1 - a, dims, half)
            send(s, a, CORE_SUM, half, core_in.at[a, s], other_core)
            product(span(fields, a, s, near, ROWS // 2), 1 - a, dims, span(terms, a, s, near, ROWS // 2))
        else:
            product(fields.at[a, s], 1 - a, dims, terms.at[a, s])
            send(s, a, CORE_SUM, half, core_in.at[a, s], other_core)
        for c in range(TILE):
            blocked[a, s, c + 1] = fields[a, s, :, c * BLK:(c + 1) * BLK]

    def core_end(s, a):
        arrived(s, a, CORE_SUM)
        half = span(terms, a, s, core * (ROWS // 2), ROWS // 2)
        add_into(half, [half, core_in.at[a, s]], ROWS // 2)
        col_ring.total(terms, col_one, col_two, s, a, COL_SUM)

    def out_mid(s, a):
        col_ring.total_mid(terms, col_one, col_two, s, a, COL_SUM)

    def out_pair(s, a):
        col_ring.total_pair(terms, col_two, col_send, col_pair, s, a, COL_SUM)

    def out_end(s, a):
        refs = col_ring.total_end(terms, col_two, col_pair, s, a, COL_SUM)
        add_into(outputs[a].at[s], refs, COL_SHARE)

    def flip(s, a):
        source = gathered.at[a, s]

        for i in range(TILE):
            flipped[a, i + 1, :, s * ROWS:(s + 1) * ROWS] = source[:, i * BLK:(i + 1) * BLK].T

    def slot(j, a):
        for i in range(j * SLOTS, (j + 1) * SLOTS):
            r, c = at[1 - a, 0, i] + 1, at[1 - a, 1, i] + 1
            left, right = (c, r) if a == 0 else (r, c)
            value = lax.dot_general(
                flipped[1 - a, left], blocked[a, :, right].reshape(TOKENS, BLK), PLAIN,
                preferred_element_type=jnp.float32,
            )
            value = (value * (1.0 / 32.0)).astype(jnp.bfloat16)
            (narrow_grad, widen_grad)[a][0, i] = value.T if a == 0 else value

    steps = {
        step.__name__: step
        for step in (
            assemble, gather, gather_mid, gather_pass, gather_core, rise, sum_mid, sum_pair, sum_end, spread_mid,
            spread_pass, spread_end, fall, core_end, out_mid, out_pair, out_end, flip, slot,
            sumb_two, sumb_one, sumb_mid, sumb_end, sprb_mid, sprb_pass, sprb_end,
        )
    }
    for index, s, a in ORDER:
        steps[STEPS[index]](s, a)
    for copy in copies.values():
        copy.wait_send()


def hand_on(*refs):
    sources, targets, sem = refs[:4], refs[4:8], refs[8]
    stores = []
    for i in range(4):
        for j in range(1 if i < 2 else CAP // SLOTS):
            part = pl.ds(j * SLOTS, SLOTS)
            source = sources[i] if i < 2 else sources[i].at[0, part]
            target = targets[i] if i < 2 else targets[i].at[0, part]
            stores.append(pltpu.make_async_copy(source, target, sem.at[i, j]))
            stores[-1].start()
    for store in stores:
        store.wait()


def local(tokens, widen_blocks, widen_pattern, narrow_blocks, narrow_pattern, cotangent):
    grouped = (STAGES, COL_SHARE, SIDE)
    anywhere, vmem = pl.BlockSpec(memory_space=pl.ANY), pl.BlockSpec(memory_space=pltpu.VMEM)
    results = (
        jax.ShapeDtypeStruct(grouped, jnp.bfloat16),
        jax.ShapeDtypeStruct(grouped, jnp.bfloat16),
        jax.ShapeDtypeStruct(widen_blocks.shape, jnp.bfloat16),
        jax.ShapeDtypeStruct(narrow_blocks.shape, jnp.bfloat16),
    )

    def room(*shape, dtype=jnp.bfloat16):
        return pltpu.VMEM((*shape, SIDE), dtype)

    outs = pl.pallas_call(
        body,
        out_shape=tuple(pltpu.VMEM(r.shape, r.dtype) for r in results),
        in_specs=[anywhere] * 6,
        out_specs=[vmem] * 4,
        scratch_shapes=[
            room(2, STAGES, ROWS),
            room(2, STAGES, ROWS),
            room(2, STAGES, ROWS),
            room(2, SIDE),
            room(2, STAGES, 2 * ROW_SHARE),
            room(2, STAGES, 4 * ROW_SHARE),
            room(2, STAGES, ROW_SHARE),
            room(2, STAGES, ROW_SHARE),
            room(2, STAGES, ROWS // 2),
            room(2, STAGES, 2 * COL_SHARE),
            room(2, STAGES, 4 * COL_SHARE),
            room(2, STAGES, COL_SHARE),
            room(2, STAGES, COL_SHARE),
            room(STAGES, ROW_SHARE, dtype=jnp.float32),
            pltpu.VMEM((CAP + 1, BLK, BLK), jnp.bfloat16),
            pltpu.VMEM((CAP + 1, BLK, BLK), jnp.bfloat16),
            pltpu.VMEM((2, TILE + 1, BLK, TOKENS), jnp.bfloat16),
            pltpu.VMEM((2, STAGES, TILE + 1, ROWS, BLK), jnp.bfloat16),
            pltpu.SMEM((2, 2, CAP), jnp.int32),
            pltpu.VMEM((2, 2 * BLK), jnp.int32),
            pltpu.SMEM((2, 2 * BLK), jnp.int32),
            pltpu.SemaphoreType.DMA((2, STAGES, COPIES)),
            pltpu.SemaphoreType.DMA((2, STAGES, COPIES)),
            pltpu.SemaphoreType.DMA((7,)),
        ],
        compiler_params=pltpu.CompilerParams(
            collective_id=0, has_side_effects=True, vmem_limit_bytes=57 * 2**20
        ),
        name="layer",
    )(
        widen_pattern[0].T, narrow_pattern[0].T, tokens.reshape(grouped), cotangent.reshape(grouped),
        widen_blocks, narrow_blocks,
    )
    outs = pl.pallas_call(
        hand_on, out_shape=results, in_specs=[vmem] * 4, out_specs=[anywhere] * 4,
        scratch_shapes=[pltpu.SemaphoreType.DMA((4, CAP // SLOTS))], name="hand_on",
    )(*(pltpu.with_memory_space_constraint(o, pltpu.VMEM) for o in outs))
    return outs[0].reshape(tokens.shape), outs[1].reshape(tokens.shape), outs[2], outs[3]


def solution(mesh):
    placed = (
        P("col", "row"),
        P("row", "col", None, None),
        P("row", "col", None),
        P("row", "col", None, None),
        P("row", "col", None),
        P("col", "row"),
    )
    return jax.shard_map(
        local,
        mesh=mesh,
        in_specs=placed,
        out_specs=(
            P("col", "row"),
            P("col", "row"),
            P("row", "col", None, None),
            P("row", "col", None, None),
        ),
        check_vma=False,
    )
```
